32 devices in a mesh: dp: 4 (over x, core), expert: 8 (over z, y).
Axes of the slice: x: 2, y: 2, z: 4, core: 2. Of those that a mesh axis runs over, the one named last changes fastest.
Arguments:
- tokens: bfloat16 [1024, 2048], P('expert', 'dp'), may hold values from -6 to 6
- cotangent: bfloat16 [1024, 2048], P('expert', 'dp'), may hold values from -6 to 6
- route: int32 [1024, 8], P('expert'), may hold values from 0 to 23, all different within a row; in each aligned block of 128 rows (0 to 127, 128 to 255, ...) at most 44 rows name the same one
- gate_prob: float32 [1024, 8], P('expert'), may hold values from 0.02 to 0.25
- replica_pick: int32 [8], replicated, may hold values from 0 to 1
- w_gate: bfloat16 [16, 1536, 2048], P('expert', 'dp'), may hold values from -0.125 to 0.125
- w_up: bfloat16 [16, 1536, 2048], P('expert', 'dp'), may hold values from -0.125 to 0.125
- w_down: bfloat16 [16, 1536, 2048], P('expert', 'dp'), may hold values from -0.15625 to 0.15625
Outputs:
- layer_out: bfloat16 [1024, 2048], P('expert', 'dp')
- token_grad: bfloat16 [1024, 2048], P('expert', 'dp')
- gate_grad: float32 [1024, 8], P('expert', 'dp')
- w_gate_grad: bfloat16 [16, 1536, 2048], P('expert', 'dp')
- w_up_grad: bfloat16 [16, 1536, 2048], P('expert', 'dp')
- w_down_grad: bfloat16 [16, 1536, 2048], P('expert', 'dp')
The draws below stay inside these ranges and needn't reach their ends.
Inputs may be any that keep to these rules, and one draw needn't show every extreme that they name: `route`: each row names 8 different copies. Among the rows of one device, in aligned blocks of 128 tokens, no copy is named more than 44 times, a bound that some block reaches.
All inputs are finite; a program needn't handle non-finite values.
Results may differ from the reference program's by a relative error of at most 0.014.
Values may be sent and summed in bfloat16 or wider, within the bound.
A program may use at most 128 MiB of HBM per device.

```python
import math
import jax
import jax.numpy as jnp
import numpy as np
from jax import lax

D = 2048
FF = 1536
TOP = 8
EXP_DEV = 2
TOK_DEV = 128
EXPERTS = 16
TOKENS = 1024
FF_DEV = 384
COPIES = 24
CAP = 44
N_DP = 4
N_EXPERT = 8


def with_ends(result, own_key, low, top_value):
    index_at = [jax.random.randint(jax.random.fold_in(own_key, axis), (), 0, length) for axis, length in enumerate(result.shape)]
    widest = result.shape.index(max(result.shape))
    beside = index_at[:widest] + [(index_at[widest] + 1) % result.shape[widest]] + index_at[widest + 1:]
    return result.at[tuple(index_at)].set(low).at[tuple(beside)].set(top_value)


def level_of(rng, extent, cuts, low, top_value):
    def one(dim, parts):
        draws = jax.random.uniform(jax.random.fold_in(jax.random.fold_in(rng, 6), dim), (parts,), jnp.float32, low / len(cuts), top_value / len(cuts))
        return jnp.repeat(jnp.exp(draws), extent[dim] // parts).reshape((-1,) + (1,) * (len(extent) - dim - 1))

    loudness = one(*cuts[0])
    for cut in cuts[1:]:
        loudness = loudness * one(*cut)
    return loudness


def shared_out(key, own, number, rows, number_of, top, most, skew):
    sequence = jax.random.permutation(key, number_of)
    crowded, usual = portions_of(number_of, rows * top, most, skew, True), portions_of(number_of, rows * top, most, skew, False)
    places = jnp.arange(number_of)

    def named(lengths, turn):
        used = int((lengths > 0).sum())
        fixed = max(1, used // 4)
        shifted = fixed + (places - fixed + turn * (used - fixed)) % max(1, number_of - fixed)
        return jnp.zeros((number_of,), jnp.int32).at[sequence[jnp.where(places < fixed, places, shifted)]].set(jnp.asarray(lengths, jnp.int32))

    lengths = jnp.where(number % 4 == 0, named(crowded, number // 4), named(usual, number - number // 4 - 1))
    mixed = jax.random.permutation(jax.random.fold_in(own, 3), number_of)
    source_of, receiver = mixed[0:number_of // 2 * 2:2], mixed[1:number_of // 2 * 2:2]
    margin = jnp.minimum(lengths[source_of] - 1, most - lengths[receiver]) // 2
    margin = jnp.where((source_of == sequence[0]) | (receiver == sequence[0]) | (lengths[receiver] == 0), 0, jnp.maximum(margin, 0))
    shifted = jax.random.randint(jax.random.fold_in(own, 4), (number_of // 2,), 0, 1 << 20) % (margin + 1)
    lengths = lengths.at[source_of].add(-shifted).at[receiver].add(shifted)
    labels = jnp.searchsorted(jnp.cumsum(lengths), jnp.arange(rows * top), side="right").astype(jnp.int32)
    listing = labels.reshape(top, rows).T
    listing = listing[jax.random.permutation(jax.random.fold_in(own, 1), rows)]
    turn = jax.random.randint(jax.random.fold_in(own, 2), (rows, 1), 0, top)
    return jnp.take_along_axis(listing, (jnp.arange(top)[None, :] + turn) % top, axis=1)


def portions_of(number_of, total, limit, skew, full):
    portions = [(1 << 20) // math.isqrt(grade ** skew) + 1 for grade in range(1, number_of + 1)]
    largest = limit if full else min(limit, max(-(-total // number_of), total * portions[0] // sum(portions)))
    least = 1 if total - largest >= number_of - 1 else 0
    holding, surplus = [largest] + [least] * (number_of - 1), total - largest - least * (number_of - 1)
    while surplus > 0:
        free = [i for i in range(1, number_of) if holding[i] < largest] or [i for i in range(1, number_of) if holding[i] < limit]
        mass, budget = sum([portions[i] for i in free]), surplus
        for i in free:
            addition = min(limit - holding[i], max(1, budget * portions[i] // mass), surplus)
            holding[i] = holding[i] + addition
            surplus = surplus - addition
    return np.array(holding)


def noise(own_key, shape, spread, limit, shards=(), kind=jnp.bfloat16):
    factor_of = level_of(own_key, shape, shards, -0.22, 0.18) if shards else 1.0
    entries = jax.random.normal(own_key, shape, jnp.float32) * spread * factor_of
    return jnp.minimum(jnp.maximum(entries, -limit), limit).astype(kind)


def setup_inputs(seed: int = 0) -> dict:
    seeds = jax.random.split(jax.random.key(seed), 9)
    tokens = noise(seeds[0], (TOKENS, D), 1.0, 6.0, ((0, 8), (1, 4)))
    cotangent = noise(seeds[1], (TOKENS, D), 1.0, 6.0, ((0, 8), (1, 4)))
    route_keys = jax.random.split(jax.random.fold_in(seeds[2], 1), TOKENS // TOK_DEV)
    route_turns = jax.random.permutation(jax.random.fold_in(seeds[2], 3), TOKENS // TOK_DEV)
    route = jax.vmap(lambda own, number: shared_out(jax.random.fold_in(seeds[2], 2), own, number, TOK_DEV, COPIES, TOP, CAP, 2))(route_keys, route_turns).reshape((TOKENS, TOP))
    gate_prob = jnp.clip(0.02 + 0.23 * jax.random.uniform(seeds[3], (TOKENS, TOP), jnp.float32) ** level_of(seeds[3], (TOKENS, TOP), ((0, 8),), -0.2, 0.2), 0.02, 0.25)
    replica_pick = with_ends(jax.random.randint(seeds[4], (N_EXPERT,), 0, EXP_DEV), jax.random.fold_in(seeds[4], 1), 0, EXP_DEV - 1).astype(jnp.int32)
    w_gate = noise(seeds[5], (EXPERTS, FF, D), D ** -0.5, 0.125, ((0, 8), (1, 4)))
    w_up = noise(seeds[6], (EXPERTS, FF, D), D ** -0.5, 0.125, ((0, 8), (1, 4)))
    w_down = noise(seeds[7], (EXPERTS, FF, D), FF ** -0.5, 0.15625, ((0, 8), (1, 4)))
    return dict(tokens=tokens, cotangent=cotangent, route=route, gate_prob=gate_prob, replica_pick=replica_pick, w_gate=w_gate, w_up=w_up, w_down=w_down)


def rounded_f32(values):
    return lax.optimization_barrier(values.astype(jnp.bfloat16)).astype(jnp.float32)


def reference(tokens, cotangent, route, gate_prob, replica_pick, w_gate, w_up, w_down):
    local_copies = EXP_DEV + 1
    slots = TOKENS * TOP
    route_rows = route.reshape(N_EXPERT, TOK_DEV * TOP)
    onehot = (route_rows[:, :, None] == jnp.arange(COPIES, dtype=jnp.int32)[None, None, :]).astype(jnp.int32)
    position = jnp.sum((jnp.cumsum(onehot, axis=1) - 1) * onehot, axis=2).astype(jnp.int32)
    source = jnp.arange(N_EXPERT, dtype=jnp.int32)[:, None]
    address = ((route_rows * N_EXPERT + source) * CAP + position).reshape(-1).astype(jnp.int32)
    slot_table = jnp.full((COPIES * N_EXPERT * CAP,), slots, jnp.int32).at[address].set(jnp.arange(slots, dtype=jnp.int32))
    slot_table = slot_table.reshape(COPIES, N_EXPERT * CAP)
    pad_tokens = jnp.concatenate([tokens, jnp.zeros((1, D), tokens.dtype)], axis=0)
    pad_cot = jnp.concatenate([cotangent, jnp.zeros((1, D), cotangent.dtype)], axis=0)
    pad_gate = jnp.concatenate([gate_prob.reshape(-1), jnp.zeros((1,), gate_prob.dtype)], axis=0)
    rows_per = N_EXPERT * CAP

    def owner_step(carry, owner_col):
        out_acc, back_acc, prob_acc = carry
        partner = (owner_col + N_EXPERT // 2) % N_EXPERT
        own_list = owner_col * local_copies + jnp.arange(EXP_DEV, dtype=jnp.int32)
        guest_copy = partner * local_copies + EXP_DEV
        copy_list = jnp.concatenate([own_list, guest_copy[None]]).astype(jnp.int32)
        slot_ids = slot_table[copy_list]
        chosen_index = replica_pick[partner]
        start = (owner_col * EXP_DEV).astype(jnp.int32)

        def stacked(weights):
            owned_w = lax.dynamic_slice_in_dim(weights, start, EXP_DEV, 0)
            extra_w = lax.dynamic_index_in_dim(owned_w, chosen_index, 0, keepdims=True)
            return jnp.concatenate([owned_w, extra_w], axis=0).astype(jnp.float32)

        gate_w = stacked(w_gate)
        up_w = stacked(w_up)
        down_w = stacked(w_down)
        token_ids = slot_ids // TOP
        rows_in = pad_tokens[token_ids].astype(jnp.float32)
        gates = pad_gate[slot_ids].astype(jnp.float32)
        rows_dy = pad_cot[token_ids].astype(jnp.float32)
        rows_cot = (gates[..., None] * rows_dy).astype(jnp.bfloat16).astype(jnp.float32)
        gate_act = jnp.einsum("cmd,cfd->cmf", rows_in, gate_w)
        up_act = jnp.einsum("cmd,cfd->cmf", rows_in, up_w)
        sigmoid_gate = jax.nn.sigmoid(gate_act)
        activated = gate_act * sigmoid_gate
        hidden = (activated * up_act).astype(jnp.bfloat16).astype(jnp.float32)
        blocks = (local_copies, N_DP, FF_DEV, D)
        hidden_blocks = hidden.reshape(local_copies, rows_per, N_DP, FF_DEV)
        out_sum = jnp.sum(rounded_f32(jnp.einsum("cmrf,crfd->crmd", hidden_blocks, down_w.reshape(blocks))), axis=1)
        d_hidden = jnp.einsum("cmd,cfd->cmf", rows_cot, down_w)
        d_gate = (d_hidden * up_act * sigmoid_gate * (1.0 + gate_act * (1.0 - sigmoid_gate))).astype(jnp.bfloat16).astype(jnp.float32)
        d_up = (d_hidden * activated).astype(jnp.bfloat16).astype(jnp.float32)
        back_blocks = jnp.einsum("cmrf,crfd->crmd", d_gate.reshape(local_copies, rows_per, N_DP, FF_DEV), gate_w.reshape(blocks))
        back_blocks = back_blocks + jnp.einsum("cmrf,crfd->crmd", d_up.reshape(local_copies, rows_per, N_DP, FF_DEV), up_w.reshape(blocks))
        back_sum = jnp.sum(rounded_f32(back_blocks), axis=1)
        grad_gate = jnp.einsum("cmf,cmd->cfd", d_gate, rows_in)
        grad_up = jnp.einsum("cmf,cmd->cfd", d_up, rows_in)
        grad_down = jnp.einsum("cmf,cmd->cfd", hidden, rows_cot)
        select = (jnp.arange(EXP_DEV, dtype=jnp.int32) == chosen_index).astype(jnp.float32)[:, None, None]
        out_gate = (grad_gate[:EXP_DEV] + select * grad_gate[EXP_DEV]).astype(jnp.bfloat16)
        out_up = (grad_up[:EXP_DEV] + select * grad_up[EXP_DEV]).astype(jnp.bfloat16)
        out_down = (grad_down[:EXP_DEV] + select * grad_down[EXP_DEV]).astype(jnp.bfloat16)
        flat_tok = token_ids.reshape(-1)
        flat_slot = slot_ids.reshape(-1)
        out_acc = out_acc.at[flat_tok].add((gates[..., None] * out_sum).reshape(-1, D))
        back_acc = back_acc.at[flat_tok].add(back_sum.reshape(-1, D))
        prob_acc = prob_acc.at[flat_slot].set(jnp.sum(rows_dy * out_sum, axis=-1).reshape(-1))
        return (out_acc, back_acc, prob_acc), (out_gate, out_up, out_down)

    start_carry = (jnp.zeros((TOKENS + 1, D), jnp.float32), jnp.zeros((TOKENS + 1, D), jnp.float32), jnp.zeros((slots + 1,), jnp.float32))
    final, grads = lax.scan(owner_step, start_carry, jnp.arange(N_EXPERT, dtype=jnp.int32))
    out_acc, back_acc, prob_acc = final
    layer_out = out_acc[:TOKENS].astype(jnp.bfloat16)
    token_grad = back_acc[:TOKENS].astype(jnp.bfloat16)
    gate_grad = prob_acc[:slots].reshape(TOKENS, TOP)
    w_gate_grad = grads[0].reshape(EXPERTS, FF, D)
    w_up_grad = grads[1].reshape(EXPERTS, FF, D)
    w_down_grad = grads[2].reshape(EXPERTS, FF, D)
    return (layer_out, token_grad, gate_grad, w_gate_grad, w_up_grad, w_down_grad)
```

```python
import jax
import jax.numpy as jnp
from jax import lax
from jax.sharding import PartitionSpec as P


def body(tokens, cotangent, route, gate_prob, replica_pick, w_gate, w_up, w_down):
    groups = lax.axis_size("expert")
    column = lax.axis_index("expert")
    tok_dev, slice_width = tokens.shape
    fanout = route.shape[1]
    owned, width, features = w_gate.shape
    local_copies = owned + 1
    copies = groups * local_copies
    capacity = tok_dev * fanout // copies + 2
    half_axis = groups // 2
    rows = groups * capacity
    total = groups * tok_dev
    f32, bf16 = jnp.float32, jnp.bfloat16

    all_route = lax.all_gather(route, "expert", axis=0, tiled=True)
    all_gate = lax.all_gather(gate_prob, "expert", axis=0, tiled=True)
    tok = lax.all_gather(tokens, "expert", axis=0, tiled=True)
    tok = lax.all_gather(tok, "dp", axis=1, tiled=True)
    cot = lax.all_gather(cotangent, "expert", axis=0, tiled=True)
    cot = lax.all_gather(cot, "dp", axis=1, tiled=True)

    partner = (column + half_axis) % groups
    own_pick = replica_pick[partner]
    select = [(own_pick == j).astype(bf16) for j in range(owned)]
    copy_ids = [column * local_copies + j for j in range(owned)] + [partner * local_copies + owned]

    route_t = all_route.T
    gate_t = all_gate.T
    hits = [route_t == c for c in copy_ids]
    member = jnp.stack([jnp.sum(h.astype(f32), axis=0) for h in hits])
    gate_of = jnp.stack([jnp.sum(jnp.where(h, gate_t, 0.0), axis=0) for h in hits])
    blocks = member.reshape(local_copies, groups, tok_dev)
    tri = (jnp.arange(tok_dev)[:, None] <= jnp.arange(tok_dev)[None, :]).astype(bf16)
    inside = jnp.einsum("cgt,tu->cgu", blocks.astype(bf16), tri, preferred_element_type=f32)
    sums = jnp.sum(blocks, axis=2)
    before = (jnp.arange(groups)[:, None] < jnp.arange(groups)[None, :]).astype(f32)
    offset = jnp.sum(sums[:, :, None] * before[None], axis=1)
    place = (inside + offset[:, :, None]).reshape(local_copies, total) - 1.0
    place = jnp.where(member > 0, place, -1.0).astype(jnp.int32)
    picks = place[:, None, :] == jnp.arange(rows, dtype=jnp.int32)[None, :, None]
    pick = picks.astype(bf16)
    gate_rows = jnp.sum(jnp.where(picks, gate_of[:, None, :], 0.0), axis=2)

    chosen = [lax.dynamic_index_in_dim(w, own_pick, 0, keepdims=True) for w in (w_gate, w_up, w_down)]
    gate_w = jnp.concatenate([w_gate, chosen[0]], axis=0)
    up_w = jnp.concatenate([w_up, chosen[1]], axis=0)
    down_w = jnp.concatenate([w_down, chosen[2]], axis=0)

    rows_in = jnp.einsum("crt,td->crd", pick, tok, preferred_element_type=f32).astype(bf16)
    gate_act = jnp.einsum("crd,cfd->crf", rows_in, gate_w, preferred_element_type=f32)
    up_act = jnp.einsum("crd,cfd->crf", rows_in, up_w, preferred_element_type=f32)
    sig = jax.nn.sigmoid(gate_act)
    activated = gate_act * sig
    hidden = activated * up_act
    g = gate_rows[:, :, None]
    hidden_g = (g * hidden).astype(bf16)
    out_rows = jnp.einsum("crf,cfd->crd", hidden_g, down_w, preferred_element_type=f32).astype(bf16)
    out_tok = jnp.einsum("crt,crd->td", pick, out_rows, preferred_element_type=f32).astype(bf16)
    out_dp = lax.psum_scatter(out_tok, "dp", scatter_dimension=1, tiled=True)
    layer_out = lax.psum_scatter(out_dp, "expert", scatter_dimension=0, tiled=True)

    rows_cot = jnp.einsum("crt,td->crd", pick, cot, preferred_element_type=f32).astype(bf16)
    back_h = jnp.einsum("crd,cfd->crf", rows_cot, down_w, preferred_element_type=f32)
    gg_rows = jnp.sum(hidden * back_h, axis=2)
    d_hidden = g * back_h
    d_gate = (d_hidden * up_act * sig * (1.0 + gate_act * (1.0 - sig))).astype(bf16)
    d_up = (d_hidden * activated).astype(bf16)
    back_rows = jnp.einsum("crf,cfd->crd", d_gate, gate_w, preferred_element_type=f32)
    back_rows = back_rows + jnp.einsum("crf,cfd->crd", d_up, up_w, preferred_element_type=f32)
    back_tok = jnp.einsum("crt,crd->td", pick, back_rows.astype(bf16), preferred_element_type=f32).astype(bf16)
    back_dp = lax.psum_scatter(back_tok, "dp", scatter_dimension=1, tiled=True)
    token_grad = lax.psum_scatter(back_dp, "expert", scatter_dimension=0, tiled=True)

    gg_tok = jnp.sum(jnp.where(picks, gg_rows[:, :, None], 0.0), axis=1)
    gg = sum(jnp.where(h, gg_tok[j][None], 0.0) for j, h in enumerate(hits))
    gg = lax.psum_scatter(gg, "expert", scatter_dimension=1, tiled=True)
    gate_grad = lax.psum_scatter(gg, "dp", scatter_dimension=0, tiled=True).T

    def weight_grad(left, right):
        parts = []
        for j in range(owned):
            both_l = jnp.concatenate([left[j], left[owned] * select[j]], axis=0)
            both_r = jnp.concatenate([right[j], right[owned]], axis=0)
            parts.append(jnp.einsum("rf,rd->fd", both_l, both_r, preferred_element_type=f32).astype(bf16))
        return jnp.stack(parts)

    return (
        layer_out,
        token_grad,
        gate_grad,
        weight_grad(d_gate, rows_in),
        weight_grad(d_up, rows_in),
        weight_grad(hidden_g, rows_cot),
    )


def solution(mesh):
    in_specs = (
        P("expert", "dp"),
        P("expert", "dp"),
        P("expert", None),
        P("expert", None),
        P(),
        P("expert", "dp", None),
        P("expert", "dp", None),
        P("expert", "dp", None),
    )
    out_specs = (
        P("expert", "dp"),
        P("expert", "dp"),
        P("expert", "dp"),
        P("expert", "dp", None),
        P("expert", "dp", None),
        P("expert", "dp", None),
    )
    return jax.shard_map(body, mesh=mesh, in_specs=in_specs, out_specs=out_specs, check_vma=False)
```

```python
import functools
import itertools
import math

import jax
import jax.numpy as jnp
from jax import lax
from jax.experimental import pallas as pl
from jax.experimental.pallas import tpu as pltpu
from jax.sharding import PartitionSpec as P

MESH = pl.DeviceIdType.MESH
GATHER_ORDERS = ((0, 1, 2, 3), (0, 2, 1, 3))
REDUCE_ORDERS = ((3, 2, 1, 0), (3, 1, 2, 0))


def lines():
    experts, dps = lax.axis_size("expert"), lax.axis_size("dp")
    along_y = math.isqrt(experts // 2)
    return (experts // along_y, along_y, dps // 2, 2)


def flipped(index, bits):
    result, bit = index, 1
    while bit <= bits:
        if bits & bit:
            result = result + bit - 2 * bit * lax.rem(lax.div(index, bit), 2)
        bit *= 2
    return result


class Place:
    def __init__(self, sizes):
        self.sizes = sizes
        self.expert, self.dp = lax.axis_index("expert"), lax.axis_index("dp")
        self.ids = list(itertools.product(*[range(s) for s in sizes]))

    def expert_of(self, d):
        return flipped(self.expert, d[0] * self.sizes[1] + d[1])

    def dp_of(self, d):
        return flipped(self.dp, d[2] * self.sizes[3] + d[3])

    def device(self, d):
        return {"dp": self.dp_of(d), "expert": self.expert_of(d)}

    def number(self, d):
        z, y, x, c = self.sizes
        return ((d[0] * y + d[1]) * x + d[2]) * c + d[3]

    def steps(self, dim):
        out = []
        for delta in range(1, self.sizes[dim]):
            step = [0, 0, 0, 0]
            step[dim] = delta
            out.append(tuple(step))
        return out

    def block(self, ref, d, rows, columns):
        return ref.at[
            pl.ds(pl.multiple_of(self.expert_of(d) * rows, rows), rows),
            pl.ds(pl.multiple_of(self.dp_of(d) * columns, columns), columns),
        ]

    def greet(self):
        barrier = pltpu.get_barrier_semaphore()
        peers = [s for dim in range(4) for s in self.steps(dim)]
        for peer in peers:
            pl.semaphore_signal(barrier, inc=1, device_id=self.device(peer), device_id_type=MESH)
        pl.semaphore_wait(barrier, len(peers))


def plus(a, b):
    return tuple(i ^ j for i, j in zip(a, b))


def remote(src, dst, send, recv, device):
    return pltpu.make_async_remote_copy(
        src_ref=src, dst_ref=dst, send_sem=send, recv_sem=recv, device_id=device, device_id_type=MESH
    )


def gather_kernel(sizes, tok_ref, cot_ref, meta_ref, tok_out, cot_out, meta_out, send, recv, own):
    place = Place(sizes)
    rows, columns = tok_ref.shape

    def view(a, ref, d):
        if a == 2:
            return ref.at[place.expert_of(d)]
        return place.block(ref, d, rows, columns)

    ins, outs = (tok_ref, cot_ref, meta_ref), (tok_out, cot_out, meta_out)
    orders = GATHER_ORDERS + ((0, 1),)
    zero = (0, 0, 0, 0)
    local = [pltpu.make_async_copy(ins[a], view(a, outs[a], zero), own.at[a]) for a in range(3)]
    for copy in local:
        copy.start()
    place.greet()
    sent = []

    def stage_of(a, d):
        return max([p for p, dim in enumerate(orders[a]) if d[dim]], default=-1)

    def forward(a, d, p):
        for step in place.steps(orders[a][p]):
            there = plus(d, step)
            n = place.number(there)
            src = ins[a] if d == zero else view(a, outs[a], d)
            copy = remote(src, view(a, outs[a], d), send.at[a, n], recv.at[a, n], place.device(step))
            copy.start()
            sent.append(copy)

    for p in range(4):
        for a in (2, 0, 1):
            if p < len(orders[a]):
                forward(a, zero, p)
    for stage in range(4):
        todo = []
        for a in (2, 0, 1):
            if stage < len(orders[a]):
                mine = [d for d in place.ids if all(d[x] == 0 for x in range(4) if x not in orders[a])]
                todo += [(i, a, d) for i, d in enumerate([d for d in mine if stage_of(a, d) == stage])]
        for _, a, d in sorted(todo, key=lambda t: t[0]):
            n = place.number(d)
            here = view(a, outs[a], d)
            remote(here, here, send.at[a, n], recv.at[a, n], place.device(place.steps(0)[0])).wait_recv()
            for p in range(stage + 1, len(orders[a])):
                forward(a, d, p)
    for copy in local:
        copy.wait()
    for copy in sent:
        copy.wait_send()


def gather_all(tokens, cotangent, meta):
    sizes = lines()
    groups, dps = lax.axis_size("expert"), lax.axis_size("dp")
    devices = groups * dps
    whole = jax.ShapeDtypeStruct((groups * tokens.shape[0], dps * tokens.shape[1]), jnp.bfloat16)
    return pl.pallas_call(
        functools.partial(gather_kernel, sizes),
        out_shape=(whole, whole, jax.ShapeDtypeStruct((groups,) + meta.shape, meta.dtype)),
        in_specs=[pl.BlockSpec(memory_space=pl.ANY)] * 3,
        out_specs=[pl.BlockSpec(memory_space=pl.ANY)] * 3,
        scratch_shapes=[
            pltpu.SemaphoreType.DMA((3, devices)),
            pltpu.SemaphoreType.DMA((3, devices)),
            pltpu.SemaphoreType.DMA((3,)),
        ],
        compiler_params=pltpu.CompilerParams(collective_id=0, has_side_effects=True),
        name="gather_all",
    )(tokens, cotangent, meta)


def reduce_kernel(sizes, out_ref, back_ref, gg_ref, layer_ref, grad_ref, prob_ref, stage, slots, gg_stage, gg_slots, send, recv, own, gg_send, gg_recv):
    place = Place(sizes)
    z_size, y_size, x_size, _ = sizes
    _, _, rows, columns = slots.shape
    refs, results = (out_ref, back_ref), (layer_ref, grad_ref)
    zero = (0, 0, 0, 0)
    kept = [d for d in place.ids if d[3] == 0]
    local = {}
    for a in range(2):
        for d in kept:
            n = place.number(d) // 2
            local[a, d] = pltpu.make_async_copy(place.block(refs[a], d, rows, columns), stage.at[a, n], own.at[a, n])
            local[a, d].start()
    place.greet()
    sent = []

    def first(a, d):
        return min([p for p, dim in enumerate(REDUCE_ORDERS[a]) if d[dim]], default=4)

    def push(a, d, p):
        dim = REDUCE_ORDERS[a][p]
        step = tuple(d[i] if i == dim else 0 for i in range(4))
        n = place.number(d)
        src = place.block(refs[a], d, rows, columns) if p == 0 else stage.at[a, n // 2]
        copy = remote(src, slots.at[a, n], send.at[a, n], recv.at[a, n], place.device(step))
        copy.start()
        sent.append(copy)

    def total(a, d, p):
        local[a, d].wait()
        value = stage[a, place.number(d) // 2].astype(jnp.float32)
        for q in range(p):
            for step in place.steps(REDUCE_ORDERS[a][q]):
                n = place.number(plus(d, step))
                remote(slots.at[a, n], slots.at[a, n], send.at[a, n], recv.at[a, n], place.device(place.steps(0)[0])).wait_recv()
                value = value + slots[a, n].astype(jnp.float32)
        return value.astype(jnp.bfloat16)

    def gg_push(src, n, step):
        copy = remote(src, gg_slots.at[n], gg_send.at[n], gg_recv.at[n], place.device(step))
        copy.start()
        sent.append(copy)

    def gg_take(n):
        remote(gg_slots.at[n], gg_slots.at[n], gg_send.at[n], gg_recv.at[n], place.device(place.steps(0)[0])).wait_recv()
        return gg_slots[n]

    experts = z_size * y_size

    def gg_step(p):
        if p == 0:
            for dz in range(z_size):
                for dy in range(1, y_size):
                    d = (dz, dy, 0, 0)
                    gg_push(gg_ref.at[place.expert_of(d)], dz * y_size + dy, (0, dy, 0, 0))
        elif p == 1:
            for dz in range(z_size):
                value = gg_ref[place.expert_of((dz, 0, 0, 0))]
                for dy in range(1, y_size):
                    value = value + gg_take(dz * y_size + dy)
                gg_stage[dz] = value
                if dz:
                    gg_push(gg_stage.at[dz], dz * y_size, (dz, 0, 0, 0))
        elif p == 2:
            value = gg_stage[0]
            for dz in range(1, z_size):
                value = value + gg_take(dz * y_size)
            gg_stage[z_size] = value
            for dx in range(1, x_size):
                gg_push(gg_stage.at[z_size], experts + dx, (0, 0, dx, 0))
        elif p == 3:
            value = gg_stage[z_size]
            for dx in range(1, x_size):
                value = value + gg_take(experts + dx)
            gg_stage[z_size + 1] = value
            gg_push(gg_stage.at[z_size + 1], experts + x_size, (0, 0, 0, 1))
        else:
            prob_ref[...] = gg_stage[z_size + 1] + gg_take(experts + x_size)

    for p in range(5):
        todo = []
        for a in range(2):
            mine = [d for d in place.ids if first(a, d) == p]
            mine.sort(key=lambda d: [d[dim] == 0 for dim in REDUCE_ORDERS[a]])
            todo += [(i, a, d) for i, d in enumerate(mine)]
        for _, a, d in sorted(todo, key=lambda t: t[0]):
            if p == 4:
                results[a][...] = total(a, d, p)
            else:
                if p:
                    stage[a, place.number(d) // 2] = total(a, d, p)
                push(a, d, p)
        gg_step(p)
    for copy in sent:
        copy.wait_send()


def reduce_all(out_tok, back_tok, gg, rows, columns):
    sizes = lines()
    devices = sizes[0] * sizes[1] * sizes[2] * sizes[3]
    block = jax.ShapeDtypeStruct((rows, columns), jnp.bfloat16)
    vmem = pl.BlockSpec(memory_space=pltpu.VMEM)
    few = sizes[0] * sizes[1] + sizes[2] + 1
    return pl.pallas_call(
        functools.partial(reduce_kernel, sizes),
        out_shape=(block, block, jax.ShapeDtypeStruct(gg.shape[1:], gg.dtype)),
        in_specs=[pl.BlockSpec(memory_space=pl.ANY)] * 2 + [vmem],
        out_specs=[vmem] * 3,
        scratch_shapes=[
            pltpu.VMEM((2, devices // 2, rows, columns), jnp.bfloat16),
            pltpu.VMEM((2, devices, rows, columns), jnp.bfloat16),
            pltpu.VMEM((sizes[0] + 2,) + gg.shape[1:], gg.dtype),
            pltpu.VMEM((few,) + gg.shape[1:], gg.dtype),
            pltpu.SemaphoreType.DMA((2, devices)),
            pltpu.SemaphoreType.DMA((2, devices)),
            pltpu.SemaphoreType.DMA((2, devices // 2)),
            pltpu.SemaphoreType.DMA((few,)),
            pltpu.SemaphoreType.DMA((few,)),
        ],
        compiler_params=pltpu.CompilerParams(
            collective_id=1, has_side_effects=True, vmem_limit_bytes=54 * 1024 * 1024
        ),
        name="reduce_all",
    )(out_tok, back_tok, gg)


def body(tokens, cotangent, route, gate_prob, replica_pick, w_gate, w_up, w_down):
    groups = lax.axis_size("expert")
    column = lax.axis_index("expert")
    tok_dev, slice_width = tokens.shape
    fanout = route.shape[1]
    owned, width, features = w_gate.shape
    local_copies = owned + 1
    copies = groups * local_copies
    capacity = tok_dev * fanout // copies + 2
    half_axis = groups // 2
    rows = groups * capacity
    total = groups * tok_dev
    f32, bf16 = jnp.float32, jnp.bfloat16

    meta = jnp.concatenate([route.T.astype(f32), gate_prob.T], axis=0)
    tok, cot, meta = gather_all(tokens, cotangent, meta)
    meta = jnp.transpose(meta, (1, 0, 2)).reshape(2 * fanout, total)
    route_t = meta[:fanout].astype(jnp.int32)
    gate_t = meta[fanout:]

    partner = (column + half_axis) % groups
    own_pick = replica_pick[partner]
    select = [(own_pick == j).astype(bf16) for j in range(owned)]
    copy_ids = [column * local_copies + j for j in range(owned)] + [partner * local_copies + owned]

    hits = [route_t == c for c in copy_ids]
    member = jnp.stack([jnp.sum(h.astype(f32), axis=0) for h in hits])
    gate_of = jnp.stack([jnp.sum(jnp.where(h, gate_t, 0.0), axis=0) for h in hits])
    blocks = member.reshape(local_copies, groups, tok_dev)
    tri = (jnp.arange(tok_dev)[:, None] <= jnp.arange(tok_dev)[None, :]).astype(bf16)
    inside = jnp.einsum("cgt,tu->cgu", blocks.astype(bf16), tri, preferred_element_type=f32)
    sums = jnp.sum(blocks, axis=2)
    before = (jnp.arange(groups)[:, None] < jnp.arange(groups)[None, :]).astype(f32)
    offset = jnp.sum(sums[:, :, None] * before[None], axis=1)
    place = (inside + offset[:, :, None]).reshape(local_copies, total) - 1.0
    place = jnp.where(member > 0, place, -1.0).astype(jnp.int32)
    picks = place[:, None, :] == jnp.arange(rows, dtype=jnp.int32)[None, :, None]
    pick = picks.astype(bf16)
    gate_rows = jnp.sum(jnp.where(picks, gate_of[:, None, :], 0.0), axis=2)

    chosen = [lax.dynamic_index_in_dim(w, own_pick, 0, keepdims=True) for w in (w_gate, w_up, w_down)]
    gate_w = jnp.concatenate([w_gate, chosen[0]], axis=0)
    up_w = jnp.concatenate([w_up, chosen[1]], axis=0)
    down_w = jnp.concatenate([w_down, chosen[2]], axis=0)

    rows_in = jnp.einsum("crt,td->crd", pick, tok, preferred_element_type=f32).astype(bf16)
    gate_act = jnp.einsum("crd,cfd->crf", rows_in, gate_w, preferred_element_type=f32)
    up_act = jnp.einsum("crd,cfd->crf", rows_in, up_w, preferred_element_type=f32)
    sig = jax.nn.sigmoid(gate_act)
    activated = gate_act * sig
    hidden = activated * up_act
    g = gate_rows[:, :, None]
    hidden_g = (g * hidden).astype(bf16)
    out_rows = jnp.einsum("crf,cfd->crd", hidden_g, down_w, preferred_element_type=f32).astype(bf16)
    out_tok = jnp.einsum("crt,crd->td", pick, out_rows, preferred_element_type=f32).astype(bf16)

    rows_cot = jnp.einsum("crt,td->crd", pick, cot, preferred_element_type=f32).astype(bf16)
    back_h = jnp.einsum("crd,cfd->crf", rows_cot, down_w, preferred_element_type=f32)
    gg_rows = jnp.sum(hidden * back_h, axis=2)
    d_hidden = g * back_h
    d_gate = (d_hidden * up_act * sig * (1.0 + gate_act * (1.0 - sig))).astype(bf16)
    d_up = (d_hidden * activated).astype(bf16)
    back_rows = jnp.einsum("crf,cfd->crd", d_gate, gate_w, preferred_element_type=f32)
    back_rows = back_rows + jnp.einsum("crf,cfd->crd", d_up, up_w, preferred_element_type=f32)
    back_tok = jnp.einsum("crt,crd->td", pick, back_rows.astype(bf16), preferred_element_type=f32).astype(bf16)

    gg_tok = jnp.sum(jnp.where(picks, gg_rows[:, :, None], 0.0), axis=1)
    gg = sum(jnp.where(h, gg_tok[j][None], 0.0) for j, h in enumerate(hits))
    gg = jnp.transpose(gg.reshape(fanout, groups, tok_dev), (1, 0, 2))
    layer_out, token_grad, gg = reduce_all(out_tok, back_tok, gg, tok_dev, slice_width)
    share = fanout // lax.axis_size("dp")
    gate_grad = lax.dynamic_slice_in_dim(gg, lax.axis_index("dp") * share, share, 0).T

    def weight_grad(left, right):
        parts = []
        for j in range(owned):
            both_l = jnp.concatenate([left[j], left[owned] * select[j]], axis=0)
            both_r = jnp.concatenate([right[j], right[owned]], axis=0)
            parts.append(jnp.einsum("rf,rd->fd", both_l, both_r, preferred_element_type=f32).astype(bf16))
        return jnp.stack(parts)

    return (
        layer_out,
        token_grad,
        gate_grad,
        weight_grad(d_gate, rows_in),
        weight_grad(d_up, rows_in),
        weight_grad(hidden_g, rows_cot),
    )


def solution(mesh):
    in_specs = (
        P("expert", "dp"),
        P("expert", "dp"),
        P("expert", None),
        P("expert", None),
        P(),
        P("expert", "dp", None),
        P("expert", "dp", None),
        P("expert", "dp", None),
    )
    out_specs = (
        P("expert", "dp"),
        P("expert", "dp"),
        P("expert", "dp"),
        P("expert", "dp", None),
        P("expert", "dp", None),
        P("expert", "dp", None),
    )
    return jax.shard_map(body, mesh=mesh, in_specs=in_specs, out_specs=out_specs, check_vma=False)
```

```python
import functools
import itertools
import math

import jax
import jax.numpy as jnp
from jax import lax
from jax.experimental import pallas as pl
from jax.experimental.pallas import tpu as pltpu
from jax.sharding import PartitionSpec as P

MESH = pl.DeviceIdType.MESH
GATHER_ORDERS = ((0, 1, 2, 3), (0, 2, 1, 3))
REDUCE_ORDERS = ((3, 2, 1, 0), (3, 1, 2, 0))


def lines():
    experts, dps = lax.axis_size("expert"), lax.axis_size("dp")
    along_y = math.isqrt(experts // 2)
    return (experts // along_y, along_y, dps // 2, 2)


def flipped(index, bits):
    result, bit = index, 1
    while bit <= bits:
        if bits & bit:
            result = result + bit - 2 * bit * lax.rem(lax.div(index, bit), 2)
        bit *= 2
    return result


class Place:
    def __init__(self, sizes):
        self.sizes = sizes
        self.expert, self.dp = lax.axis_index("expert"), lax.axis_index("dp")
        self.ids = list(itertools.product(*[range(s) for s in sizes]))

    def expert_of(self, d):
        return flipped(self.expert, d[0] * self.sizes[1] + d[1])

    def dp_of(self, d):
        return flipped(self.dp, d[2] * self.sizes[3] + d[3])

    def device(self, d):
        return {"dp": self.dp_of(d), "expert": self.expert_of(d)}

    def number(self, d):
        z, y, x, c = self.sizes
        return ((d[0] * y + d[1]) * x + d[2]) * c + d[3]

    def steps(self, dim):
        out = []
        for delta in range(1, self.sizes[dim]):
            step = [0, 0, 0, 0]
            step[dim] = delta
            out.append(tuple(step))
        return out

    def block(self, ref, d, rows, columns):
        return ref.at[
            pl.ds(pl.multiple_of(self.expert_of(d) * rows, rows), rows),
            pl.ds(pl.multiple_of(self.dp_of(d) * columns, columns), columns),
        ]

    def greet(self):
        barrier = pltpu.get_barrier_semaphore()
        peers = [s for dim in range(4) for s in self.steps(dim)]
        for peer in peers:
            pl.semaphore_signal(barrier, inc=1, device_id=self.device(peer), device_id_type=MESH)
        pl.semaphore_wait(barrier, len(peers))


def plus(a, b):
    return tuple(i ^ j for i, j in zip(a, b))


def remote(src, dst, send, recv, device):
    return pltpu.make_async_remote_copy(
        src_ref=src, dst_ref=dst, send_sem=send, recv_sem=recv, device_id=device, device_id_type=MESH
    )


def gather_kernel(sizes, tok_ref, cot_ref, meta_ref, tok_out, cot_out, meta_out, send, recv, own):
    place = Place(sizes)
    rows, columns = tok_ref.shape

    def view(a, ref, d):
        if a == 2:
            return ref.at[place.expert_of(d)]
        return place.block(ref, d, rows, columns)

    ins, outs = (tok_ref, cot_ref, meta_ref), (tok_out, cot_out, meta_out)
    orders = GATHER_ORDERS + ((0, 1),)
    zero = (0, 0, 0, 0)
    local = [pltpu.make_async_copy(ins[a], view(a, outs[a], zero), own.at[a]) for a in range(3)]
    for copy in local:
        copy.start()
    place.greet()
    sent = []

    def stage_of(a, d):
        return max([p for p, dim in enumerate(orders[a]) if d[dim]], default=-1)

    def forward(a, d, p):
        for step in place.steps(orders[a][p]):
            there = plus(d, step)
            n = place.number(there)
            src = ins[a] if d == zero else view(a, outs[a], d)
            copy = remote(src, view(a, outs[a], d), send.at[a, n], recv.at[a, n], place.device(step))
            copy.start()
            sent.append(copy)

    for p in range(4):
        for a in (2, 0, 1):
            if p < len(orders[a]):
                forward(a, zero, p)
    for stage in range(4):
        todo = []
        for a in (2, 0, 1):
            if stage < len(orders[a]):
                mine = [d for d in place.ids if all(d[x] == 0 for x in range(4) if x not in orders[a])]
                todo += [(i, a, d) for i, d in enumerate([d for d in mine if stage_of(a, d) == stage])]
        for _, a, d in sorted(todo, key=lambda t: t[0]):
            n = place.number(d)
            here = view(a, outs[a], d)
            remote(here, here, send.at[a, n], recv.at[a, n], place.device(place.steps(0)[0])).wait_recv()
            for p in range(stage + 1, len(orders[a])):
                forward(a, d, p)
    for copy in local:
        copy.wait()
    for copy in sent:
        copy.wait_send()


def gather_all(tokens, cotangent, meta):
    sizes = lines()
    groups, dps = lax.axis_size("expert"), lax.axis_size("dp")
    devices = groups * dps
    whole = jax.ShapeDtypeStruct((groups * tokens.shape[0], dps * tokens.shape[1]), jnp.bfloat16)
    return pl.pallas_call(
        functools.partial(gather_kernel, sizes),
        out_shape=(whole, whole, jax.ShapeDtypeStruct((groups,) + meta.shape, meta.dtype)),
        in_specs=[pl.BlockSpec(memory_space=pl.ANY)] * 3,
        out_specs=[pl.BlockSpec(memory_space=pl.ANY)] * 3,
        scratch_shapes=[
            pltpu.SemaphoreType.DMA((3, devices)),
            pltpu.SemaphoreType.DMA((3, devices)),
            pltpu.SemaphoreType.DMA((3,)),
        ],
        compiler_params=pltpu.CompilerParams(collective_id=0, has_side_effects=True),
        name="gather_all",
    )(tokens, cotangent, meta)


def reduce_kernel(sizes, out_ref, back_ref, gg_ref, layer_ref, grad_ref, prob_ref, stage, slots, gg_stage, gg_slots, send, recv, own, gg_send, gg_recv):
    place = Place(sizes)
    z_size, y_size, x_size, _ = sizes
    _, _, rows, columns = slots.shape
    refs, results = (out_ref, back_ref), (layer_ref, grad_ref)
    zero = (0, 0, 0, 0)
    kept = [d for d in place.ids if d[3] == 0]
    local = {}
    for a in range(2):
        for d in kept:
            n = place.number(d) // 2
            local[a, d] = pltpu.make_async_copy(place.block(refs[a], d, rows, columns), stage.at[a, n], own.at[a, n])
            local[a, d].start()
    place.greet()
    sent = []

    def first(a, d):
        return min([p for p, dim in enumerate(REDUCE_ORDERS[a]) if d[dim]], default=4)

    def push(a, d, p):
        dim = REDUCE_ORDERS[a][p]
        step = tuple(d[i] if i == dim else 0 for i in range(4))
        n = place.number(d)
        src = place.block(refs[a], d, rows, columns) if p == 0 else stage.at[a, n // 2]
        copy = remote(src, slots.at[a, n], send.at[a, n], recv.at[a, n], place.device(step))
        copy.start()
        sent.append(copy)

    def total(a, d, p):
        local[a, d].wait()
        value = stage[a, place.number(d) // 2].astype(jnp.float32)
        for q in range(p):
            for step in place.steps(REDUCE_ORDERS[a][q]):
                n = place.number(plus(d, step))
                remote(slots.at[a, n], slots.at[a, n], send.at[a, n], recv.at[a, n], place.device(place.steps(0)[0])).wait_recv()
                value = value + slots[a, n].astype(jnp.float32)
        return value.astype(jnp.bfloat16)

    def gg_push(src, n, step):
        copy = remote(src, gg_slots.at[n], gg_send.at[n], gg_recv.at[n], place.device(step))
        copy.start()
        sent.append(copy)

    def gg_take(n):
        remote(gg_slots.at[n], gg_slots.at[n], gg_send.at[n], gg_recv.at[n], place.device(place.steps(0)[0])).wait_recv()
        return gg_slots[n]

    experts = z_size * y_size

    def gg_step(p):
        if p == 0:
            for dz in range(z_size):
                for dy in range(1, y_size):
                    d = (dz, dy, 0, 0)
                    gg_push(gg_ref.at[place.expert_of(d)], dz * y_size + dy, (0, dy, 0, 0))
        elif p == 1:
            for dz in range(z_size):
                value = gg_ref[place.expert_of((dz, 0, 0, 0))]
                for dy in range(1, y_size):
                    value = value + gg_take(dz * y_size + dy)
                gg_stage[dz] = value
                if dz:
                    gg_push(gg_stage.at[dz], dz * y_size, (dz, 0, 0, 0))
        elif p == 2:
            value = gg_stage[0]
            for dz in range(1, z_size):
                value = value + gg_take(dz * y_size)
            gg_stage[z_size] = value
            for dx in range(1, x_size):
                gg_push(gg_stage.at[z_size], experts + dx, (0, 0, dx, 0))
        elif p == 3:
            value = gg_stage[z_size]
            for dx in range(1, x_size):
                value = value + gg_take(experts + dx)
            gg_stage[z_size + 1] = value
            gg_push(gg_stage.at[z_size + 1], experts + x_size, (0, 0, 0, 1))
        else:
            prob_ref[...] = gg_stage[z_size + 1] + gg_take(experts + x_size)

    for p in range(5):
        todo = []
        for a in range(2):
            mine = [d for d in place.ids if first(a, d) == p]
            mine.sort(key=lambda d: [d[dim] == 0 for dim in REDUCE_ORDERS[a]])
            todo += [(i, a, d) for i, d in enumerate(mine)]
        for _, a, d in sorted(todo, key=lambda t: t[0]):
            if p == 4:
                results[a][...] = total(a, d, p)
            else:
                if p:
                    stage[a, place.number(d) // 2] = total(a, d, p)
                push(a, d, p)
        gg_step(p)
    for copy in sent:
        copy.wait_send()


def reduce_all(out_tok, back_tok, gg, rows, columns):
    sizes = lines()
    devices = sizes[0] * sizes[1] * sizes[2] * sizes[3]
    block = jax.ShapeDtypeStruct((rows, columns), jnp.bfloat16)
    vmem = pl.BlockSpec(memory_space=pltpu.VMEM)
    few = sizes[0] * sizes[1] + sizes[2] + 1
    return pl.pallas_call(
        functools.partial(reduce_kernel, sizes),
        out_shape=(block, block, jax.ShapeDtypeStruct(gg.shape[1:], gg.dtype)),
        in_specs=[pl.BlockSpec(memory_space=pl.ANY)] * 2 + [vmem],
        out_specs=[vmem] * 3,
        scratch_shapes=[
            pltpu.VMEM((2, devices // 2, rows, columns), jnp.bfloat16),
            pltpu.VMEM((2, devices, rows, columns), jnp.bfloat16),
            pltpu.VMEM((sizes[0] + 2,) + gg.shape[1:], gg.dtype),
            pltpu.VMEM((few,) + gg.shape[1:], gg.dtype),
            pltpu.SemaphoreType.DMA((2, devices)),
            pltpu.SemaphoreType.DMA((2, devices)),
            pltpu.SemaphoreType.DMA((2, devices // 2)),
            pltpu.SemaphoreType.DMA((few,)),
            pltpu.SemaphoreType.DMA((few,)),
        ],
        compiler_params=pltpu.CompilerParams(
            collective_id=1, has_side_effects=True, vmem_limit_bytes=54 * 1024 * 1024
        ),
        name="reduce_all",
    )(out_tok, back_tok, gg)


def finish_kernel(
    sizes, hid_ref, dg_ref, du_ref, sel_ref, pt_ref, gg_ref, rin_ref, rcot_ref, wg_ref, wu_ref, wd_ref, cg_ref, cu_ref, cd_ref,
    layer_ref, grad_ref, prob_ref, wgg_ref, wug_ref, wdg_ref,
    stage, slots, wide, rows_buf, made, tiles, gg_stage, gg_slots, send, recv, loaded, stored, gg_send, gg_recv,
):
    place = Place(sizes)
    z_size, y_size, x_size, _ = sizes
    _, _, rows, columns = slots.shape
    results = (layer_ref, grad_ref)
    owned = wg_ref.shape[0]
    slot_rows = hid_ref.shape[1]
    tokens = pt_ref.shape[0]
    f32, bf16 = jnp.float32, jnp.bfloat16

    loads = []
    for i, (own, guest) in enumerate(((wd_ref, cd_ref), (wg_ref, cg_ref), (wu_ref, cu_ref))):
        loads.append(pltpu.make_async_copy(own, wide.at[i, pl.ds(0, owned)], loaded.at[2 * i]))
        loads.append(pltpu.make_async_copy(guest, wide.at[i, pl.ds(owned, 1)], loaded.at[2 * i + 1]))
    loads.append(pltpu.make_async_copy(rin_ref, rows_buf.at[0], loaded.at[6]))
    loads.append(pltpu.make_async_copy(rcot_ref, rows_buf.at[1], loaded.at[7]))
    for copy in loads:
        copy.start()
    barrier = pltpu.get_barrier_semaphore()
    peers = [s for dim in range(4) for s in place.steps(dim)]
    for peer in peers:
        pl.semaphore_signal(barrier, inc=1, device_id=place.device(peer), device_id_type=MESH)
    sent = []

    def granule(a, d):
        return stage.at[a, d[2] * 2 + d[3], pl.ds(pl.multiple_of(place.expert_of(d) * rows, rows), rows)]

    def first(a, d):
        return min([p for p, dim in enumerate(REDUCE_ORDERS[a]) if d[dim]], default=4)

    def make(a, d):
        cols = pl.ds(pl.multiple_of(place.dp_of(d) * columns, columns), columns)
        for c in range(owned + 1):
            if a == 0:
                part = jnp.dot(hid_ref[c], wide[0, c, :, cols], preferred_element_type=f32)
            else:
                part = jnp.dot(dg_ref[c], wide[1, c, :, cols], preferred_element_type=f32)
                part = part + jnp.dot(du_ref[c], wide[2, c, :, cols], preferred_element_type=f32)
            made[pl.ds(c * slot_rows, slot_rows)] = part.astype(bf16)
        step = 2 * rows

        @pl.loop(0, tokens // step)
        def _(i):
            at = pl.ds(pl.multiple_of(i * step, step), step)
            sums = jnp.dot(pt_ref[at], made[...], preferred_element_type=f32)
            stage[a, d[2] * 2 + d[3], at] = sums.astype(bf16)

    def push(a, d, p):
        dim = REDUCE_ORDERS[a][p]
        step = tuple(d[i] if i == dim else 0 for i in range(4))
        n = place.number(d)
        copy = remote(granule(a, d), slots.at[a, n], send.at[a, n], recv.at[a, n], place.device(step))
        copy.start()
        sent.append(copy)

    def total(a, d, p):
        value = granule(a, d)[...].astype(f32)
        for q in range(p):
            for step in place.steps(REDUCE_ORDERS[a][q]):
                n = place.number(plus(d, step))
                remote(slots.at[a, n], slots.at[a, n], send.at[a, n], recv.at[a, n], place.device(place.steps(0)[0])).wait_recv()
                value = value + slots[a, n].astype(f32)
        return value.astype(bf16)

    def gg_push(src, n, step):
        copy = remote(src, gg_slots.at[n], gg_send.at[n], gg_recv.at[n], place.device(step))
        copy.start()
        sent.append(copy)

    def gg_take(n):
        remote(gg_slots.at[n], gg_slots.at[n], gg_send.at[n], gg_recv.at[n], place.device(place.steps(0)[0])).wait_recv()
        return gg_slots[n]

    experts = z_size * y_size

    def gg_step(p):
        if p == 0:
            for dz in range(z_size):
                for dy in range(1, y_size):
                    d = (dz, dy, 0, 0)
                    gg_push(gg_ref.at[place.expert_of(d)], dz * y_size + dy, (0, dy, 0, 0))
        elif p == 1:
            for dz in range(z_size):
                value = gg_ref[place.expert_of((dz, 0, 0, 0))]
                for dy in range(1, y_size):
                    value = value + gg_take(dz * y_size + dy)
                gg_stage[dz] = value
                if dz:
                    gg_push(gg_stage.at[dz], dz * y_size, (dz, 0, 0, 0))
        elif p == 2:
            value = gg_stage[0]
            for dz in range(1, z_size):
                value = value + gg_take(dz * y_size)
            gg_stage[z_size] = value
            for dx in range(1, x_size):
                gg_push(gg_stage.at[z_size], experts + dx, (0, 0, dx, 0))
        elif p == 3:
            value = gg_stage[z_size]
            for dx in range(1, x_size):
                value = value + gg_take(experts + dx)
            gg_stage[z_size + 1] = value
            gg_push(gg_stage.at[z_size + 1], experts + x_size, (0, 0, 0, 1))
        else:
            prob_ref[...] = gg_stage[z_size + 1] + gg_take(experts + x_size)

    lefts, outs = (hid_ref, dg_ref, du_ref), (wdg_ref, wgg_ref, wug_ref)
    stores = []

    def weight_grad(task):
        w, j = divmod(task, owned)
        if task == 0:
            loads[6].wait()
            loads[7].wait()
        if task >= 2:
            stores[task - 2].wait()
        slot, right = task % 2, 1 if w == 0 else 0
        step = 512

        @pl.loop(0, wide.shape[3] // step)
        def _(i):
            at = pl.ds(pl.multiple_of(i * step, step), step)
            dims = (((0,), (0,)), ((), ()))
            value = lax.dot_general(lefts[w][j], rows_buf[right, j, :, at], dims, preferred_element_type=f32)
            value = value + lax.dot_general(sel_ref[w, j], rows_buf[right, owned, :, at], dims, preferred_element_type=f32)
            tiles[slot, :, at] = value.astype(bf16)

        copy = pltpu.make_async_copy(tiles.at[slot], outs[w].at[j], stored.at[task])
        copy.start()
        stores.append(copy)

    waited = False
    slices = sorted({d[2:] for d in place.ids}, key=lambda s: (s[1] == 0, s[0] == 0))
    for s in slices:
        for a in range(2):
            if s == slices[0]:
                for copy in loads[:2] if a == 0 else loads[2:6]:
                    copy.wait()
            make(a, (0, 0) + s)
            if not waited:
                pl.semaphore_wait(barrier, len(peers))
                waited = True
                gg_step(0)
            if s[1]:
                mine = [d for d in place.ids if d[2:] == s]
                mine.sort(key=lambda d: [d[dim] == 0 for dim in REDUCE_ORDERS[a]])
                for d in mine:
                    push(a, d, 0)
            elif a == 0 and s[0]:
                for d in place.ids:
                    if d[2:] == s:
                        n = granule(a, d)
                        n[...] = total(a, d, 1)
                        push(a, d, 1)
    tasks = 3 * owned
    spread = {1: range(0, tasks // 2), 2: range(tasks // 2, tasks - 1), 3: range(tasks - 1, tasks)}
    for p in range(1, 5):
        todo = []
        for a in range(2):
            mine = [d for d in place.ids if first(a, d) == p and not (p == 1 and a == 0)]
            mine.sort(key=lambda d: [d[dim] == 0 for dim in REDUCE_ORDERS[a]])
            todo += [(i, a, d) for i, d in enumerate(mine)]
        for _, a, d in sorted(todo, key=lambda t: t[0]):
            if p == 4:
                results[a][...] = total(a, d, p)
            else:
                n = granule(a, d)
                n[...] = total(a, d, p)
                push(a, d, p)
        gg_step(p)
        for task in spread.get(p, ()):
            weight_grad(task)
    for copy in stores[-2:]:
        copy.wait()
    for copy in sent:
        copy.wait_send()


def finish(hidden, d_gate, d_up, select, pick_t, gg, rows_in, rows_cot, w_gate, w_up, w_down, chosen, rows, columns):
    sizes = lines()
    devices = sizes[0] * sizes[1] * sizes[2] * sizes[3]
    owned, width, features = w_gate.shape
    sel = jnp.stack([jnp.stack([left[owned] * s for s in select]) for left in (hidden, d_gate, d_up)])
    block = jax.ShapeDtypeStruct((rows, columns), jnp.bfloat16)
    grad = jax.ShapeDtypeStruct(w_gate.shape, jnp.bfloat16)
    vmem, anywhere = pl.BlockSpec(memory_space=pltpu.VMEM), pl.BlockSpec(memory_space=pl.ANY)
    few = sizes[0] * sizes[1] + sizes[2] + 1
    dps = sizes[2] * sizes[3]
    bf16 = jnp.bfloat16
    return pl.pallas_call(
        functools.partial(finish_kernel, sizes),
        out_shape=(block, block, jax.ShapeDtypeStruct(gg.shape[1:], gg.dtype), grad, grad, grad),
        in_specs=[vmem] * 6 + [anywhere] * 8,
        out_specs=[vmem] * 3 + [anywhere] * 3,
        scratch_shapes=[
            pltpu.VMEM((2, dps, pick_t.shape[0], columns), bf16),
            pltpu.VMEM((2, devices, rows, columns), bf16),
            pltpu.VMEM((3, owned + 1, width, features), bf16),
            pltpu.VMEM((2,) + rows_in.shape, bf16),
            pltpu.VMEM((pick_t.shape[1], columns), bf16),
            pltpu.VMEM((2, width, features), bf16),
            pltpu.VMEM((sizes[0] + 2,) + gg.shape[1:], gg.dtype),
            pltpu.VMEM((few,) + gg.shape[1:], gg.dtype),
            pltpu.SemaphoreType.DMA((2, devices)),
            pltpu.SemaphoreType.DMA((2, devices)),
            pltpu.SemaphoreType.DMA((8,)),
            pltpu.SemaphoreType.DMA((3 * owned,)),
            pltpu.SemaphoreType.DMA((few,)),
            pltpu.SemaphoreType.DMA((few,)),
        ],
        compiler_params=pltpu.CompilerParams(
            collective_id=1, has_side_effects=True, vmem_limit_bytes=60 * 1024 * 1024
        ),
        name="finish",
    )(hidden, d_gate, d_up, sel, pick_t, gg, rows_in, rows_cot, w_gate, w_up, w_down, *chosen)


def body(tokens, cotangent, route, gate_prob, replica_pick, w_gate, w_up, w_down):
    groups = lax.axis_size("expert")
    column = lax.axis_index("expert")
    tok_dev, slice_width = tokens.shape
    fanout = route.shape[1]
    owned, width, features = w_gate.shape
    local_copies = owned + 1
    copies = groups * local_copies
    capacity = tok_dev * fanout // copies + 2
    half_axis = groups // 2
    rows = groups * capacity
    total = groups * tok_dev
    f32, bf16 = jnp.float32, jnp.bfloat16

    meta = jnp.concatenate([route.T.astype(f32), gate_prob.T], axis=0)
    tok, cot, meta = gather_all(tokens, cotangent, meta)
    meta = jnp.transpose(meta, (1, 0, 2)).reshape(2 * fanout, total)
    route_t = meta[:fanout].astype(jnp.int32)
    gate_t = meta[fanout:]

    partner = (column + half_axis) % groups
    own_pick = replica_pick[partner]
    select = [(own_pick == j).astype(bf16) for j in range(owned)]
    copy_ids = [column * local_copies + j for j in range(owned)] + [partner * local_copies + owned]

    hits = [route_t == c for c in copy_ids]
    member = jnp.stack([jnp.sum(h.astype(f32), axis=0) for h in hits])
    gate_of = jnp.stack([jnp.sum(jnp.where(h, gate_t, 0.0), axis=0) for h in hits])
    blocks = member.reshape(local_copies, groups, tok_dev)
    tri = (jnp.arange(tok_dev)[:, None] <= jnp.arange(tok_dev)[None, :]).astype(bf16)
    inside = jnp.einsum("cgt,tu->cgu", blocks.astype(bf16), tri, preferred_element_type=f32)
    sums = jnp.sum(blocks, axis=2)
    before = (jnp.arange(groups)[:, None] < jnp.arange(groups)[None, :]).astype(f32)
    offset = jnp.sum(sums[:, :, None] * before[None], axis=1)
    place = (inside + offset[:, :, None]).reshape(local_copies, total) - 1.0
    place = jnp.where(member > 0, place, -1.0).astype(jnp.int32)
    picks = place[:, None, :] == jnp.arange(rows, dtype=jnp.int32)[None, :, None]
    pick = picks.astype(bf16)
    gate_rows = jnp.sum(jnp.where(picks, gate_of[:, None, :], 0.0), axis=2)

    chosen = [lax.dynamic_index_in_dim(w, own_pick, 0, keepdims=True) for w in (w_gate, w_up, w_down)]
    gate_w = jnp.concatenate([w_gate, chosen[0]], axis=0)
    up_w = jnp.concatenate([w_up, chosen[1]], axis=0)
    down_w = jnp.concatenate([w_down, chosen[2]], axis=0)

    rows_in = jnp.einsum("crt,td->crd", pick, tok, preferred_element_type=f32).astype(bf16)
    gate_act = jnp.einsum("crd,cfd->crf", rows_in, gate_w, preferred_element_type=f32)
    up_act = jnp.einsum("crd,cfd->crf", rows_in, up_w, preferred_element_type=f32)
    sig = jax.nn.sigmoid(gate_act)
    activated = gate_act * sig
    hidden = activated * up_act
    g = gate_rows[:, :, None]
    hidden_g = (g * hidden).astype(bf16)

    rows_cot = jnp.einsum("crt,td->crd", pick, cot, preferred_element_type=f32).astype(bf16)
    back_h = jnp.einsum("crd,cfd->crf", rows_cot, down_w, preferred_element_type=f32)
    gg_rows = jnp.sum(hidden * back_h, axis=2)
    d_hidden = g * back_h
    d_gate = (d_hidden * up_act * sig * (1.0 + gate_act * (1.0 - sig))).astype(bf16)
    d_up = (d_hidden * activated).astype(bf16)
    gg_tok = jnp.sum(jnp.where(picks, gg_rows[:, :, None], 0.0), axis=1)
    gg = sum(jnp.where(h, gg_tok[j][None], 0.0) for j, h in enumerate(hits))
    gg = jnp.transpose(gg.reshape(fanout, groups, tok_dev), (1, 0, 2))
    share = fanout // lax.axis_size("dp")
    if 8 * total * features > 1 << 25:
        out_rows = jnp.einsum("crf,cfd->crd", hidden_g, down_w, preferred_element_type=f32).astype(bf16)
        out_tok = jnp.einsum("crt,crd->td", pick, out_rows, preferred_element_type=f32).astype(bf16)
        back_rows = jnp.einsum("crf,cfd->crd", d_gate, gate_w, preferred_element_type=f32)
        back_rows = back_rows + jnp.einsum("crf,cfd->crd", d_up, up_w, preferred_element_type=f32)
        back_tok = jnp.einsum("crt,crd->td", pick, back_rows.astype(bf16), preferred_element_type=f32).astype(bf16)
        layer_out, token_grad, gg = reduce_all(out_tok, back_tok, gg, tok_dev, slice_width)

        def weight_grad(left, right):
            parts = []
            for j in range(owned):
                both_l = jnp.concatenate([left[j], left[owned] * select[j]], axis=0)
                both_r = jnp.concatenate([right[j], right[owned]], axis=0)
                parts.append(jnp.einsum("rf,rd->fd", both_l, both_r, preferred_element_type=f32).astype(bf16))
            return jnp.stack(parts)

        grads = weight_grad(d_gate, rows_in), weight_grad(d_up, rows_in), weight_grad(hidden_g, rows_cot)
    else:
        slot = jnp.where(place < 0, -1, place + rows * jnp.arange(local_copies, dtype=jnp.int32)[:, None]).T
        every = jnp.arange(local_copies * rows, dtype=jnp.int32)[None, :]
        pick_t = sum((slot[:, j : j + 1] == every).astype(bf16) for j in range(local_copies))
        layer_out, token_grad, gg, *grads = finish(
            hidden_g, d_gate, d_up, select, pick_t, gg, rows_in, rows_cot, w_gate, w_up, w_down, chosen, tok_dev, slice_width
        )
    gate_grad = lax.dynamic_slice_in_dim(gg, lax.axis_index("dp") * share, share, 0).T
    return (layer_out, token_grad, gate_grad, *grads)


def solution(mesh):
    in_specs = (
        P("expert", "dp"),
        P("expert", "dp"),
        P("expert", None),
        P("expert", None),
        P(),
        P("expert", "dp", None),
        P("expert", "dp", None),
        P("expert", "dp", None),
    )
    out_specs = (
        P("expert", "dp"),
        P("expert", "dp"),
        P("expert", "dp"),
        P("expert", "dp", None),
        P("expert", "dp", None),
        P("expert", "dp", None),
    )
    return jax.shard_map(body, mesh=mesh, in_specs=in_specs, out_specs=out_specs, check_vma=False)
```

```python
import functools
import itertools
import math

import jax
import jax.numpy as jnp
from jax import lax
from jax.experimental import pallas as pl
from jax.experimental.pallas import tpu as pltpu
from jax.sharding import PartitionSpec as P

MESH = pl.DeviceIdType.MESH
GATHER_ORDERS = ((0, 1, 2, 3), (0, 2, 1, 3))
REDUCE_ORDERS = ((3, 2, 1, 0), (3, 1, 2, 0))


def lines():
    experts, dps = lax.axis_size("expert"), lax.axis_size("dp")
    along_y = math.isqrt(experts // 2)
    return (experts // along_y, along_y, dps // 2, 2)


def flipped(index, bits):
    result, bit = index, 1
    while bit <= bits:
        if bits & bit:
            result = result + bit - 2 * bit * lax.rem(lax.div(index, bit), 2)
        bit *= 2
    return result


class Place:
    def __init__(self, sizes):
        self.sizes = sizes
        self.expert, self.dp = lax.axis_index("expert"), lax.axis_index("dp")
        self.ids = list(itertools.product(*[range(s) for s in sizes]))

    def expert_of(self, d):
        return flipped(self.expert, d[0] * self.sizes[1] + d[1])

    def dp_of(self, d):
        return flipped(self.dp, d[2] * self.sizes[3] + d[3])

    def device(self, d):
        return {"dp": self.dp_of(d), "expert": self.expert_of(d)}

    def number(self, d):
        z, y, x, c = self.sizes
        return ((d[0] * y + d[1]) * x + d[2]) * c + d[3]

    def steps(self, dim):
        out = []
        for delta in range(1, self.sizes[dim]):
            step = [0, 0, 0, 0]
            step[dim] = delta
            out.append(tuple(step))
        return out

    def block(self, ref, d, rows, columns):
        return ref.at[
            pl.ds(pl.multiple_of(self.expert_of(d) * rows, rows), rows),
            pl.ds(pl.multiple_of(self.dp_of(d) * columns, columns), columns),
        ]

    def greet(self):
        barrier = pltpu.get_barrier_semaphore()
        peers = [s for dim in range(4) for s in self.steps(dim)]
        for peer in peers:
            pl.semaphore_signal(barrier, inc=1, device_id=self.device(peer), device_id_type=MESH)
        pl.semaphore_wait(barrier, len(peers))


def plus(a, b):
    return tuple(i ^ j for i, j in zip(a, b))


def remote(src, dst, send, recv, device):
    return pltpu.make_async_remote_copy(
        src_ref=src, dst_ref=dst, send_sem=send, recv_sem=recv, device_id=device, device_id_type=MESH
    )


def gather_kernel(sizes, tok_ref, cot_ref, meta_ref, tok_out, cot_out, meta_out, send, recv, own):
    place = Place(sizes)
    rows, columns = tok_ref.shape

    def view(a, ref, d):
        if a == 2:
            return ref.at[place.expert_of(d)]
        return place.block(ref, d, rows, columns)

    ins, outs = (tok_ref, cot_ref, meta_ref), (tok_out, cot_out, meta_out)
    orders = GATHER_ORDERS + ((0, 1),)
    zero = (0, 0, 0, 0)
    local = [pltpu.make_async_copy(ins[a], view(a, outs[a], zero), own.at[a]) for a in range(3)]
    for copy in local:
        copy.start()
    place.greet()
    sent = []

    def stage_of(a, d):
        return max([p for p, dim in enumerate(orders[a]) if d[dim]], default=-1)

    def forward(a, d, p):
        for step in place.steps(orders[a][p]):
            there = plus(d, step)
            n = place.number(there)
            src = ins[a] if d == zero else view(a, outs[a], d)
            copy = remote(src, view(a, outs[a], d), send.at[a, n], recv.at[a, n], place.device(step))
            copy.start()
            sent.append(copy)

    for p in range(4):
        for a in (2, 0, 1):
            if p < len(orders[a]):
                forward(a, zero, p)
    for stage in range(4):
        todo = []
        for a in (2, 0, 1):
            if stage < len(orders[a]):
                mine = [d for d in place.ids if all(d[x] == 0 for x in range(4) if x not in orders[a])]
                todo += [(i, a, d) for i, d in enumerate([d for d in mine if stage_of(a, d) == stage])]
        for _, a, d in sorted(todo, key=lambda t: t[0]):
            n = place.number(d)
            here = view(a, outs[a], d)
            remote(here, here, send.at[a, n], recv.at[a, n], place.device(place.steps(0)[0])).wait_recv()
            for p in range(stage + 1, len(orders[a])):
                forward(a, d, p)
    for copy in local:
        copy.wait()
    for copy in sent:
        copy.wait_send()


def gather_all(tokens, cotangent, meta):
    sizes = lines()
    groups, dps = lax.axis_size("expert"), lax.axis_size("dp")
    devices = groups * dps
    whole = jax.ShapeDtypeStruct((groups * tokens.shape[0], dps * tokens.shape[1]), jnp.bfloat16)
    return pl.pallas_call(
        functools.partial(gather_kernel, sizes),
        out_shape=(whole, whole, jax.ShapeDtypeStruct((groups,) + meta.shape, meta.dtype)),
        in_specs=[pl.BlockSpec(memory_space=pl.ANY)] * 3,
        out_specs=[pl.BlockSpec(memory_space=pl.ANY)] * 3,
        scratch_shapes=[
            pltpu.SemaphoreType.DMA((3, devices)),
            pltpu.SemaphoreType.DMA((3, devices)),
            pltpu.SemaphoreType.DMA((3,)),
        ],
        compiler_params=pltpu.CompilerParams(collective_id=0, has_side_effects=True),
        name="gather_all",
    )(tokens, cotangent, meta)


def gather_rows_kernel(sizes, tok_ref, cot_ref, meta_ref, rin_ref, rcot_ref, meta_out, tok_out, cot_out, pick, picked, send, recv, own, stored):
    place = Place(sizes)
    rows, columns = tok_ref.shape

    def view(a, ref, d):
        if a == 2:
            return ref.at[place.expert_of(d)]
        return place.block(ref, d, rows, columns)

    ins, outs = (tok_ref, cot_ref, meta_ref), (tok_out, cot_out, meta_out)
    orders = GATHER_ORDERS + ((0, 1),)
    zero = (0, 0, 0, 0)
    local = [pltpu.make_async_copy(ins[a], view(a, outs[a], zero), own.at[a]) for a in range(3)]
    for copy in local:
        copy.start()
    place.greet()
    sent = []

    def stage_of(a, d):
        return max([p for p, dim in enumerate(orders[a]) if d[dim]], default=-1)

    def forward(a, d, p):
        for step in place.steps(orders[a][p]):
            there = plus(d, step)
            n = place.number(there)
            src = ins[a] if d == zero else view(a, outs[a], d)
            copy = remote(src, view(a, outs[a], d), send.at[a, n], recv.at[a, n], place.device(step))
            copy.start()
            sent.append(copy)

    for p in range(4):
        for a in (2, 0, 1):
            if p < len(orders[a]):
                forward(a, zero, p)
    copies, slot_rows, total = pick.shape
    groups, lines_of, tok_dev = meta_out.shape
    half = sizes[0] * sizes[1] // 2
    f32, bf16 = jnp.float32, jnp.bfloat16
    stores = []

    def build():
        partner = lax.rem(place.expert + half, groups)
        names = [place.expert * copies + c for c in range(copies - 1)] + [partner * copies + copies - 1]
        earlier = lax.broadcasted_iota(jnp.int32, (tok_dev, tok_dev), 0)
        later = lax.broadcasted_iota(jnp.int32, (tok_dev, tok_dev), 1)
        tri = (earlier <= later).astype(f32).astype(bf16)
        slot = lax.broadcasted_iota(jnp.int32, (slot_rows, tok_dev), 0).astype(f32)
        for c in range(copies):
            name = names[c].astype(f32)
            before = jnp.zeros((1, 1), f32)
            for g in range(groups):
                hit = meta_out[g][: lines_of // 2] == name
                member = jnp.sum(hit.astype(f32), axis=0, keepdims=True)
                wide = jnp.broadcast_to(member, (16, tok_dev)).astype(bf16)
                inside = jnp.dot(wide, tri, preferred_element_type=f32)[:1]
                at = jnp.where(member > 0, inside + before - 1.0, -1.0)
                pick[c, :, pl.ds(g * tok_dev, tok_dev)] = (slot == at).astype(f32).astype(bf16)
                before = before + jnp.sum(member, axis=1, keepdims=True)

    def choose(a, d):
        cols = pl.ds(pl.multiple_of(place.dp_of(d) * columns, columns), columns)

        @pl.loop(0, copies)
        def _(c):
            rows_of = jnp.dot(pick[c], outs[a][:, cols], preferred_element_type=f32)
            picked[a, c, :, cols] = rows_of.astype(bf16)

        target = (rin_ref, rcot_ref)[a]
        copy = pltpu.make_async_copy(picked.at[a, :, :, cols], target.at[:, :, cols], stored.at[a, d[2] * 2 + d[3]])
        copy.start()
        stores.append(copy)

    def take(a, d):
        n = place.number(d)
        here = view(a, outs[a], d)
        remote(here, here, send.at[a, n], recv.at[a, n], place.device(place.steps(0)[0])).wait_recv()

    for stage in range(3):
        todo = []
        for a in (2, 0, 1):
            if stage < len(orders[a]):
                mine = [d for d in place.ids if all(d[x] == 0 for x in range(4) if x not in orders[a])]
                todo += [(i, a, d) for i, d in enumerate([d for d in mine if stage_of(a, d) == stage])]
        for _, a, d in sorted(todo, key=lambda t: t[0]):
            take(a, d)
            for p in range(stage + 1, len(orders[a])):
                forward(a, d, p)
        if stage == 1:
            for copy in local:
                copy.wait()
            build()
            choose(0, zero)
        if stage == 2:
            choose(1, zero)
            for dx in range(1, sizes[2]):
                choose(0, (0, 0, dx, 0))
                choose(1, (0, 0, dx, 0))
    for dx in range(sizes[2]):
        for a in range(2):
            for d in place.ids:
                if d[2:] == (dx, 1):
                    take(a, d)
            choose(a, (0, 0, dx, 1))
    for copy in stores:
        copy.wait()
    for copy in sent:
        copy.wait_send()


def gather_rows(tokens, cotangent, meta, copies, slot_rows):
    sizes = lines()
    groups, dps = lax.axis_size("expert"), lax.axis_size("dp")
    devices = groups * dps
    total, features = groups * tokens.shape[0], dps * tokens.shape[1]
    picked = (copies, slot_rows, features)
    out = jax.ShapeDtypeStruct(picked, jnp.bfloat16)
    anywhere = pl.BlockSpec(memory_space=pl.ANY)
    return pl.pallas_call(
        functools.partial(gather_rows_kernel, sizes),
        out_shape=(out, out, jax.ShapeDtypeStruct((groups,) + meta.shape, meta.dtype)),
        in_specs=[anywhere] * 3,
        out_specs=[anywhere] * 2 + [pl.BlockSpec(memory_space=pltpu.VMEM)],
        scratch_shapes=[
            pltpu.VMEM((total, features), jnp.bfloat16),
            pltpu.VMEM((total, features), jnp.bfloat16),
            pltpu.VMEM((copies, slot_rows, total), jnp.bfloat16),
            pltpu.VMEM((2,) + picked, jnp.bfloat16),
            pltpu.SemaphoreType.DMA((3, devices)),
            pltpu.SemaphoreType.DMA((3, devices)),
            pltpu.SemaphoreType.DMA((3,)),
            pltpu.SemaphoreType.DMA((2, dps)),
        ],
        compiler_params=pltpu.CompilerParams(
            collective_id=0, has_side_effects=True, vmem_limit_bytes=40 * 1024 * 1024
        ),
        name="gather_rows",
    )(tokens, cotangent, meta)


def reduce_kernel(sizes, out_ref, back_ref, gg_ref, layer_ref, grad_ref, prob_ref, stage, slots, gg_stage, gg_slots, send, recv, own, gg_send, gg_recv):
    place = Place(sizes)
    z_size, y_size, x_size, _ = sizes
    _, _, rows, columns = slots.shape
    refs, results = (out_ref, back_ref), (layer_ref, grad_ref)
    zero = (0, 0, 0, 0)
    kept = [d for d in place.ids if d[3] == 0]
    local = {}
    for a in range(2):
        for d in kept:
            n = place.number(d) // 2
            local[a, d] = pltpu.make_async_copy(place.block(refs[a], d, rows, columns), stage.at[a, n], own.at[a, n])
            local[a, d].start()
    place.greet()
    sent = []

    def first(a, d):
        return min([p for p, dim in enumerate(REDUCE_ORDERS[a]) if d[dim]], default=4)

    def push(a, d, p):
        dim = REDUCE_ORDERS[a][p]
        step = tuple(d[i] if i == dim else 0 for i in range(4))
        n = place.number(d)
        src = place.block(refs[a], d, rows, columns) if p == 0 else stage.at[a, n // 2]
        copy = remote(src, slots.at[a, n], send.at[a, n], recv.at[a, n], place.device(step))
        copy.start()
        sent.append(copy)

    def total(a, d, p):
        local[a, d].wait()
        value = stage[a, place.number(d) // 2].astype(jnp.float32)
        for q in range(p):
            for step in place.steps(REDUCE_ORDERS[a][q]):
                n = place.number(plus(d, step))
                remote(slots.at[a, n], slots.at[a, n], send.at[a, n], recv.at[a, n], place.device(place.steps(0)[0])).wait_recv()
                value = value + slots[a, n].astype(jnp.float32)
        return value.astype(jnp.bfloat16)

    def gg_push(src, n, step):
        copy = remote(src, gg_slots.at[n], gg_send.at[n], gg_recv.at[n], place.device(step))
        copy.start()
        sent.append(copy)

    def gg_take(n):
        remote(gg_slots.at[n], gg_slots.at[n], gg_send.at[n], gg_recv.at[n], place.device(place.steps(0)[0])).wait_recv()
        return gg_slots[n]

    experts = z_size * y_size

    def gg_step(p):
        if p == 0:
            for dz in range(z_size):
                for dy in range(1, y_size):
                    d = (dz, dy, 0, 0)
                    gg_push(gg_ref.at[place.expert_of(d)], dz * y_size + dy, (0, dy, 0, 0))
        elif p == 1:
            for dz in range(z_size):
                value = gg_ref[place.expert_of((dz, 0, 0, 0))]
                for dy in range(1, y_size):
                    value = value + gg_take(dz * y_size + dy)
                gg_stage[dz] = value
                if dz:
                    gg_push(gg_stage.at[dz], dz * y_size, (dz, 0, 0, 0))
        elif p == 2:
            value = gg_stage[0]
            for dz in range(1, z_size):
                value = value + gg_take(dz * y_size)
            gg_stage[z_size] = value
            for dx in range(1, x_size):
                gg_push(gg_stage.at[z_size], experts + dx, (0, 0, dx, 0))
        elif p == 3:
            value = gg_stage[z_size]
            for dx in range(1, x_size):
                value = value + gg_take(experts + dx)
            gg_stage[z_size + 1] = value
            gg_push(gg_stage.at[z_size + 1], experts + x_size, (0, 0, 0, 1))
        else:
            prob_ref[...] = gg_stage[z_size + 1] + gg_take(experts + x_size)

    for p in range(5):
        todo = []
        for a in range(2):
            mine = [d for d in place.ids if first(a, d) == p]
            mine.sort(key=lambda d: [d[dim] == 0 for dim in REDUCE_ORDERS[a]])
            todo += [(i, a, d) for i, d in enumerate(mine)]
        for _, a, d in sorted(todo, key=lambda t: t[0]):
            if p == 4:
                results[a][...] = total(a, d, p)
            else:
                if p:
                    stage[a, place.number(d) // 2] = total(a, d, p)
                push(a, d, p)
        gg_step(p)
    for copy in sent:
        copy.wait_send()


def reduce_all(out_tok, back_tok, gg, rows, columns):
    sizes = lines()
    devices = sizes[0] * sizes[1] * sizes[2] * sizes[3]
    block = jax.ShapeDtypeStruct((rows, columns), jnp.bfloat16)
    vmem = pl.BlockSpec(memory_space=pltpu.VMEM)
    few = sizes[0] * sizes[1] + sizes[2] + 1
    return pl.pallas_call(
        functools.partial(reduce_kernel, sizes),
        out_shape=(block, block, jax.ShapeDtypeStruct(gg.shape[1:], gg.dtype)),
        in_specs=[pl.BlockSpec(memory_space=pl.ANY)] * 2 + [vmem],
        out_specs=[vmem] * 3,
        scratch_shapes=[
            pltpu.VMEM((2, devices // 2, rows, columns), jnp.bfloat16),
            pltpu.VMEM((2, devices, rows, columns), jnp.bfloat16),
            pltpu.VMEM((sizes[0] + 2,) + gg.shape[1:], gg.dtype),
            pltpu.VMEM((few,) + gg.shape[1:], gg.dtype),
            pltpu.SemaphoreType.DMA((2, devices)),
            pltpu.SemaphoreType.DMA((2, devices)),
            pltpu.SemaphoreType.DMA((2, devices // 2)),
            pltpu.SemaphoreType.DMA((few,)),
            pltpu.SemaphoreType.DMA((few,)),
        ],
        compiler_params=pltpu.CompilerParams(
            collective_id=1, has_side_effects=True, vmem_limit_bytes=54 * 1024 * 1024
        ),
        name="reduce_all",
    )(out_tok, back_tok, gg)


def finish_kernel(
    sizes, hid_ref, dg_ref, du_ref, sel_ref, pt_ref, gg_ref, rin_ref, rcot_ref, wg_ref, wu_ref, wd_ref, cg_ref, cu_ref, cd_ref,
    layer_ref, grad_ref, prob_ref, wgg_ref, wug_ref, wdg_ref,
    stage, slots, wide, rows_buf, made, tiles, gg_stage, gg_slots, send, recv, loaded, stored, gg_send, gg_recv,
):
    place = Place(sizes)
    z_size, y_size, x_size, _ = sizes
    _, _, rows, columns = slots.shape
    results = (layer_ref, grad_ref)
    owned = wg_ref.shape[0]
    slot_rows = hid_ref.shape[1]
    tokens = pt_ref.shape[0]
    f32, bf16 = jnp.float32, jnp.bfloat16

    loads = []
    for i, (own, guest) in enumerate(((wd_ref, cd_ref), (wg_ref, cg_ref), (wu_ref, cu_ref))):
        loads.append(pltpu.make_async_copy(own, wide.at[i, pl.ds(0, owned)], loaded.at[2 * i]))
        loads.append(pltpu.make_async_copy(guest, wide.at[i, pl.ds(owned, 1)], loaded.at[2 * i + 1]))
    loads.append(pltpu.make_async_copy(rin_ref, rows_buf.at[0], loaded.at[6]))
    loads.append(pltpu.make_async_copy(rcot_ref, rows_buf.at[1], loaded.at[7]))
    for copy in loads:
        copy.start()
    barrier = pltpu.get_barrier_semaphore()
    peers = [s for dim in range(4) for s in place.steps(dim)]
    for peer in peers:
        pl.semaphore_signal(barrier, inc=1, device_id=place.device(peer), device_id_type=MESH)
    sent = []

    def granule(a, d):
        return stage.at[a, d[2] * 2 + d[3], pl.ds(pl.multiple_of(place.expert_of(d) * rows, rows), rows)]

    def first(a, d):
        return min([p for p, dim in enumerate(REDUCE_ORDERS[a]) if d[dim]], default=4)

    def make(a, d):
        cols = pl.ds(pl.multiple_of(place.dp_of(d) * columns, columns), columns)
        for c in range(owned + 1):
            if a == 0:
                part = jnp.dot(hid_ref[c], wide[0, c, :, cols], preferred_element_type=f32)
            else:
                part = jnp.dot(dg_ref[c], wide[1, c, :, cols], preferred_element_type=f32)
                part = part + jnp.dot(du_ref[c], wide[2, c, :, cols], preferred_element_type=f32)
            made[pl.ds(c * slot_rows, slot_rows)] = part.astype(bf16)
        step = 2 * rows

        @pl.loop(0, tokens // step)
        def _(i):
            at = pl.ds(pl.multiple_of(i * step, step), step)
            sums = jnp.dot(pt_ref[at], made[...], preferred_element_type=f32)
            stage[a, d[2] * 2 + d[3], at] = sums.astype(bf16)

    def push(a, d, p):
        dim = REDUCE_ORDERS[a][p]
        step = tuple(d[i] if i == dim else 0 for i in range(4))
        n = place.number(d)
        copy = remote(granule(a, d), slots.at[a, n], send.at[a, n], recv.at[a, n], place.device(step))
        copy.start()
        sent.append(copy)

    def total(a, d, p):
        value = granule(a, d)[...].astype(f32)
        for q in range(p):
            for step in place.steps(REDUCE_ORDERS[a][q]):
                n = place.number(plus(d, step))
                remote(slots.at[a, n], slots.at[a, n], send.at[a, n], recv.at[a, n], place.device(place.steps(0)[0])).wait_recv()
                value = value + slots[a, n].astype(f32)
        return value.astype(bf16)

    def gg_push(src, n, step):
        copy = remote(src, gg_slots.at[n], gg_send.at[n], gg_recv.at[n], place.device(step))
        copy.start()
        sent.append(copy)

    def gg_take(n):
        remote(gg_slots.at[n], gg_slots.at[n], gg_send.at[n], gg_recv.at[n], place.device(place.steps(0)[0])).wait_recv()
        return gg_slots[n]

    experts = z_size * y_size

    def gg_step(p):
        if p == 0:
            for dz in range(z_size):
                for dy in range(1, y_size):
                    d = (dz, dy, 0, 0)
                    gg_push(gg_ref.at[place.expert_of(d)], dz * y_size + dy, (0, dy, 0, 0))
        elif p == 1:
            for dz in range(z_size):
                value = gg_ref[place.expert_of((dz, 0, 0, 0))]
                for dy in range(1, y_size):
                    value = value + gg_take(dz * y_size + dy)
                gg_stage[dz] = value
                if dz:
                    gg_push(gg_stage.at[dz], dz * y_size, (dz, 0, 0, 0))
        elif p == 2:
            value = gg_stage[0]
            for dz in range(1, z_size):
                value = value + gg_take(dz * y_size)
            gg_stage[z_size] = value
            for dx in range(1, x_size):
                gg_push(gg_stage.at[z_size], experts + dx, (0, 0, dx, 0))
        elif p == 3:
            value = gg_stage[z_size]
            for dx in range(1, x_size):
                value = value + gg_take(experts + dx)
            gg_stage[z_size + 1] = value
            gg_push(gg_stage.at[z_size + 1], experts + x_size, (0, 0, 0, 1))
        else:
            prob_ref[...] = gg_stage[z_size + 1] + gg_take(experts + x_size)

    lefts, outs = (hid_ref, dg_ref, du_ref), (wdg_ref, wgg_ref, wug_ref)
    stores = []

    def weight_grad(task):
        w, j = divmod(task, owned)
        if task == 0:
            loads[6].wait()
            loads[7].wait()
        if task >= 2:
            stores[task - 2].wait()
        slot, right = task % 2, 1 if w == 0 else 0
        step = 512

        @pl.loop(0, wide.shape[3] // step)
        def _(i):
            at = pl.ds(pl.multiple_of(i * step, step), step)
            dims = (((0,), (0,)), ((), ()))
            value = lax.dot_general(lefts[w][j], rows_buf[right, j, :, at], dims, preferred_element_type=f32)
            value = value + lax.dot_general(sel_ref[w, j], rows_buf[right, owned, :, at], dims, preferred_element_type=f32)
            tiles[slot, :, at] = value.astype(bf16)

        copy = pltpu.make_async_copy(tiles.at[slot], outs[w].at[j], stored.at[task])
        copy.start()
        stores.append(copy)

    waited = False
    slices = sorted({d[2:] for d in place.ids}, key=lambda s: (s[1] == 0, s[0] == 0))
    for s in slices:
        for a in range(2):
            if s == slices[0]:
                for copy in loads[:2] if a == 0 else loads[2:6]:
                    copy.wait()
            make(a, (0, 0) + s)
            if not waited:
                pl.semaphore_wait(barrier, len(peers))
                waited = True
                gg_step(0)
            if s[1]:
                mine = [d for d in place.ids if d[2:] == s]
                mine.sort(key=lambda d: [d[dim] == 0 for dim in REDUCE_ORDERS[a]])
                for d in mine:
                    push(a, d, 0)
            elif a == 0 and s[0]:
                for d in place.ids:
                    if d[2:] == s:
                        n = granule(a, d)
                        n[...] = total(a, d, 1)
                        push(a, d, 1)
    tasks = 3 * owned
    spread = {1: range(0, tasks // 2), 2: range(tasks // 2, tasks - 1), 3: range(tasks - 1, tasks)}
    for p in range(1, 5):
        todo = []
        for a in range(2):
            mine = [d for d in place.ids if first(a, d) == p and not (p == 1 and a == 0)]
            mine.sort(key=lambda d: [d[dim] == 0 for dim in REDUCE_ORDERS[a]])
            todo += [(i, a, d) for i, d in enumerate(mine)]
        for _, a, d in sorted(todo, key=lambda t: t[0]):
            if p == 4:
                results[a][...] = total(a, d, p)
            else:
                n = granule(a, d)
                n[...] = total(a, d, p)
                push(a, d, p)
        gg_step(p)
        for task in spread.get(p, ()):
            weight_grad(task)
    for copy in stores[-2:]:
        copy.wait()
    for copy in sent:
        copy.wait_send()


def finish(hidden, d_gate, d_up, select, pick_t, gg, rows_in, rows_cot, w_gate, w_up, w_down, chosen, rows, columns):
    sizes = lines()
    devices = sizes[0] * sizes[1] * sizes[2] * sizes[3]
    owned, width, features = w_gate.shape
    sel = jnp.stack([jnp.stack([left[owned] * s for s in select]) for left in (hidden, d_gate, d_up)])
    block = jax.ShapeDtypeStruct((rows, columns), jnp.bfloat16)
    grad = jax.ShapeDtypeStruct(w_gate.shape, jnp.bfloat16)
    vmem, anywhere = pl.BlockSpec(memory_space=pltpu.VMEM), pl.BlockSpec(memory_space=pl.ANY)
    few = sizes[0] * sizes[1] + sizes[2] + 1
    dps = sizes[2] * sizes[3]
    bf16 = jnp.bfloat16
    return pl.pallas_call(
        functools.partial(finish_kernel, sizes),
        out_shape=(block, block, jax.ShapeDtypeStruct(gg.shape[1:], gg.dtype), grad, grad, grad),
        in_specs=[vmem] * 6 + [anywhere] * 8,
        out_specs=[vmem] * 3 + [anywhere] * 3,
        scratch_shapes=[
            pltpu.VMEM((2, dps, pick_t.shape[0], columns), bf16),
            pltpu.VMEM((2, devices, rows, columns), bf16),
            pltpu.VMEM((3, owned + 1, width, features), bf16),
            pltpu.VMEM((2,) + rows_in.shape, bf16),
            pltpu.VMEM((pick_t.shape[1], columns), bf16),
            pltpu.VMEM((2, width, features), bf16),
            pltpu.VMEM((sizes[0] + 2,) + gg.shape[1:], gg.dtype),
            pltpu.VMEM((few,) + gg.shape[1:], gg.dtype),
            pltpu.SemaphoreType.DMA((2, devices)),
            pltpu.SemaphoreType.DMA((2, devices)),
            pltpu.SemaphoreType.DMA((8,)),
            pltpu.SemaphoreType.DMA((3 * owned,)),
            pltpu.SemaphoreType.DMA((few,)),
            pltpu.SemaphoreType.DMA((few,)),
        ],
        compiler_params=pltpu.CompilerParams(
            collective_id=1, has_side_effects=True, vmem_limit_bytes=60 * 1024 * 1024
        ),
        name="finish",
    )(hidden, d_gate, d_up, sel, pick_t, gg, rows_in, rows_cot, w_gate, w_up, w_down, *chosen)


def body(tokens, cotangent, route, gate_prob, replica_pick, w_gate, w_up, w_down):
    groups = lax.axis_size("expert")
    column = lax.axis_index("expert")
    tok_dev, slice_width = tokens.shape
    fanout = route.shape[1]
    owned, width, features = w_gate.shape
    local_copies = owned + 1
    copies = groups * local_copies
    capacity = tok_dev * fanout // copies + 2
    half_axis = groups // 2
    rows = groups * capacity
    total = groups * tok_dev
    f32, bf16 = jnp.float32, jnp.bfloat16

    meta = jnp.concatenate([route.T.astype(f32), gate_prob.T], axis=0)
    fits = 8 * total * features <= 1 << 25
    if fits:
        rows_in, rows_cot, meta = gather_rows(tokens, cotangent, meta, local_copies, rows)
    else:
        tok, cot, meta = gather_all(tokens, cotangent, meta)
    meta, replica_pick = lax.optimization_barrier((meta, replica_pick))
    meta = jnp.transpose(meta, (1, 0, 2)).reshape(2 * fanout, total)
    route_t = meta[:fanout].astype(jnp.int32)
    gate_t = meta[fanout:]

    partner = (column + half_axis) % groups
    own_pick = replica_pick[partner]
    select = [(own_pick == j).astype(bf16) for j in range(owned)]
    copy_ids = [column * local_copies + j for j in range(owned)] + [partner * local_copies + owned]

    hits = [route_t == c for c in copy_ids]
    member = jnp.stack([jnp.sum(h.astype(f32), axis=0) for h in hits])
    gate_of = jnp.stack([jnp.sum(jnp.where(h, gate_t, 0.0), axis=0) for h in hits])
    blocks = member.reshape(local_copies, groups, tok_dev)
    tri = (jnp.arange(tok_dev)[:, None] <= jnp.arange(tok_dev)[None, :]).astype(bf16)
    inside = jnp.einsum("cgt,tu->cgu", blocks.astype(bf16), tri, preferred_element_type=f32)
    sums = jnp.sum(blocks, axis=2)
    before = (jnp.arange(groups)[:, None] < jnp.arange(groups)[None, :]).astype(f32)
    offset = jnp.sum(sums[:, :, None] * before[None], axis=1)
    place = (inside + offset[:, :, None]).reshape(local_copies, total) - 1.0
    place = jnp.where(member > 0, place, -1.0).astype(jnp.int32)
    picks = place[:, None, :] == jnp.arange(rows, dtype=jnp.int32)[None, :, None]
    pick = picks.astype(bf16)
    gate_rows = jnp.sum(jnp.where(picks, gate_of[:, None, :], 0.0), axis=2)

    chosen = [lax.dynamic_index_in_dim(w, own_pick, 0, keepdims=True) for w in (w_gate, w_up, w_down)]
    gate_w = jnp.concatenate([w_gate, chosen[0]], axis=0)
    up_w = jnp.concatenate([w_up, chosen[1]], axis=0)
    down_w = jnp.concatenate([w_down, chosen[2]], axis=0)

    if not fits:
        rows_in = jnp.einsum("crt,td->crd", pick, tok, preferred_element_type=f32).astype(bf16)
        rows_cot = jnp.einsum("crt,td->crd", pick, cot, preferred_element_type=f32).astype(bf16)
    gate_act = jnp.einsum("crd,cfd->crf", rows_in, gate_w, preferred_element_type=f32)
    up_act = jnp.einsum("crd,cfd->crf", rows_in, up_w, preferred_element_type=f32)
    sig = jax.nn.sigmoid(gate_act)
    activated = gate_act * sig
    hidden = activated * up_act
    g = gate_rows[:, :, None]
    hidden_g = (g * hidden).astype(bf16)

    back_h = jnp.einsum("crd,cfd->crf", rows_cot, down_w, preferred_element_type=f32)
    gg_rows = jnp.sum(hidden * back_h, axis=2)
    d_hidden = g * back_h
    d_gate = (d_hidden * up_act * sig * (1.0 + gate_act * (1.0 - sig))).astype(bf16)
    d_up = (d_hidden * activated).astype(bf16)
    gg_tok = jnp.sum(jnp.where(picks, gg_rows[:, :, None], 0.0), axis=1)
    gg = sum(jnp.where(h, gg_tok[j][None], 0.0) for j, h in enumerate(hits))
    gg = jnp.transpose(gg.reshape(fanout, groups, tok_dev), (1, 0, 2))
    share = fanout // lax.axis_size("dp")
    if not fits:
        out_rows = jnp.einsum("crf,cfd->crd", hidden_g, down_w, preferred_element_type=f32).astype(bf16)
        out_tok = jnp.einsum("crt,crd->td", pick, out_rows, preferred_element_type=f32).astype(bf16)
        back_rows = jnp.einsum("crf,cfd->crd", d_gate, gate_w, preferred_element_type=f32)
        back_rows = back_rows + jnp.einsum("crf,cfd->crd", d_up, up_w, preferred_element_type=f32)
        back_tok = jnp.einsum("crt,crd->td", pick, back_rows.astype(bf16), preferred_element_type=f32).astype(bf16)
        layer_out, token_grad, gg = reduce_all(out_tok, back_tok, gg, tok_dev, slice_width)

        def weight_grad(left, right):
            parts = []
            for j in range(owned):
                both_l = jnp.concatenate([left[j], left[owned] * select[j]], axis=0)
                both_r = jnp.concatenate([right[j], right[owned]], axis=0)
                parts.append(jnp.einsum("rf,rd->fd", both_l, both_r, preferred_element_type=f32).astype(bf16))
            return jnp.stack(parts)

        grads = weight_grad(d_gate, rows_in), weight_grad(d_up, rows_in), weight_grad(hidden_g, rows_cot)
    else:
        slot = jnp.where(place < 0, -1, place + rows * jnp.arange(local_copies, dtype=jnp.int32)[:, None]).T
        every = jnp.arange(local_copies * rows, dtype=jnp.int32)[None, :]
        pick_t = sum((slot[:, j : j + 1] == every).astype(bf16) for j in range(local_copies))
        layer_out, token_grad, gg, *grads = finish(
            hidden_g, d_gate, d_up, select, pick_t, gg, rows_in, rows_cot, w_gate, w_up, w_down, chosen, tok_dev, slice_width
        )
    gate_grad = lax.dynamic_slice_in_dim(gg, lax.axis_index("dp") * share, share, 0).T
    return (layer_out, token_grad, gate_grad, *grads)


def solution(mesh):
    in_specs = (
        P("expert", "dp"),
        P("expert", "dp"),
        P("expert", None),
        P("expert", None),
        P(),
        P("expert", "dp", None),
        P("expert", "dp", None),
        P("expert", "dp", None),
    )
    out_specs = (
        P("expert", "dp"),
        P("expert", "dp"),
        P("expert", "dp"),
        P("expert", "dp", None),
        P("expert", "dp", None),
        P("expert", "dp", None),
    )
    return jax.shard_map(body, mesh=mesh, in_specs=in_specs, out_specs=out_specs, check_vma=False)
```
